128 devices in a mesh: row: 8 (over z, core), col: 16 (over x, y).
Axes of the slice: x: 4, y: 4, z: 4, core: 2. Of those that a mesh axis runs over, the one named last changes fastest.
Arguments:
- coords: float32 [16, 65536], replicated, may hold values from -8 to 8
- panel: bfloat16 [65536, 128], P(('row', 'col')), may hold values from -6 to 6
- mixing: float32 [128, 64], replicated, may hold values from -0.5 to 0.5
- owners: int32 [8192, 1], P(('row', 'col')), may hold values from 0 to 127; in each aligned block of 64 rows (0 to 63, 64 to 127, ...) no two rows name the same one
- leaf_picks: int32 [8192, 2], P(('row', 'col')), may hold values from 0 to 1
Outputs:
- bases: bfloat16 [256, 16384], P(('row', 'col'))
- couplings: float32 [8192, 4096], P(('row', 'col'))
The draws below stay inside these ranges and needn't reach their ends.
Inputs may be any that keep to these rules, and one draw needn't show every extreme that they name: `owners`: among the 64 pairs of one device, no device is named more than 1 times, so the 64 pairs of a device name 64 distinct devices; every device is named somewhere.
All inputs are finite; a program needn't handle non-finite values.
Results may differ from the reference program's by a relative error of at most 0.011.
Values may be sent and summed in bfloat16 or wider, within the bound.
A program may use at most 64 MiB of HBM per device.

```python
import math
import jax
import jax.numpy as jnp
import numpy as np
from jax import lax

PT_DEV = 512
LEAF = 256
RANK = 64
SKETCH = 128
DIM = 16
NSWEEPS = 6
CAP = 1
NPTS = 65536
LEAVES_DEV = 2
NLEAVES = 256
PAIRS_DEV = 64
NPAIRS = 8192
DEVICES = 128


def draw_coords(key, part):
    key_center = jax.random.fold_in(key, 101)
    key_offset = jax.random.fold_in(key, 202)
    key_jitter = jax.random.fold_in(key, 303)
    centers = 0.7071 * jax.random.normal(key_center, (DIM, DEVICES), jnp.float32)
    offsets = 0.5 * jax.random.normal(key_offset, (DIM, NLEAVES), jnp.float32)
    jitter = 0.5 * jax.random.normal(key_jitter, (DIM, NPTS), jnp.float32)
    coords = jnp.repeat(centers, PT_DEV, axis=1) + jnp.repeat(offsets, LEAF, axis=1) + jitter
    return jnp.clip(coords, -8.0, 8.0)


def plant(result, rng, low, largest):
    shape = result.shape
    index_at = [jax.random.randint(jax.random.fold_in(rng, axis), (), 0, shape[axis]) for axis in range(len(shape))]
    result = result.at[tuple(index_at)].set(low)
    longest = shape.index(max(shape))
    index_at[longest] = (index_at[longest] + 1) % shape[longest]
    return result.at[tuple(index_at)].set(largest)


def level_of(own_key, dims, cuts, least, top_value):
    gain, own = 1.0, jax.random.fold_in(own_key, 6)
    for axis_at, parts in cuts:
        draws = jnp.exp(jax.random.uniform(jax.random.fold_in(own, axis_at), (parts,), jnp.float32, least / len(cuts), top_value / len(cuts)))
        gain = gain * jnp.repeat(draws, dims[axis_at] // parts).reshape([-1 if axis == axis_at else 1 for axis in range(len(dims))])
    return gain


def deal_out(stream_key, own, number, rows, count, top, reach, skew):
    ranking = jax.random.permutation(stream_key, count)
    packed, ordinary = portions_of(count, rows * top, reach, skew, True), portions_of(count, rows * top, reach, skew, False)
    places = jnp.arange(count)

    def named(lengths, offset_by):
        used = int((lengths > 0).sum())
        fixed = max(1, used // 4)
        passed = fixed + (places - fixed + offset_by * (used - fixed)) % max(1, count - fixed)
        return jnp.zeros((count,), jnp.int32).at[ranking[jnp.where(places < fixed, places, passed)]].set(jnp.asarray(lengths, jnp.int32))

    lengths = jnp.where(number % 4 == 0, named(packed, number // 4), named(ordinary, number - number // 4 - 1))
    mixed = jax.random.permutation(jax.random.fold_in(own, 3), count)
    source_of, sink = mixed[0:count // 2 * 2:2], mixed[1:count // 2 * 2:2]
    room = jnp.minimum(lengths[source_of] - 1, reach - lengths[sink]) // 2
    room = jnp.where((source_of == ranking[0]) | (sink == ranking[0]) | (lengths[sink] == 0), 0, jnp.maximum(room, 0))
    passed = jax.random.randint(jax.random.fold_in(own, 4), (count // 2,), 0, 1 << 20) % (room + 1)
    lengths = lengths.at[source_of].add(-passed).at[sink].add(passed)
    members = jnp.searchsorted(jnp.cumsum(lengths), jnp.arange(rows * top), side="right").astype(jnp.int32)
    grid = members.reshape(top, rows).T
    grid = grid[jax.random.permutation(jax.random.fold_in(own, 1), rows)]
    offset_by = jax.random.randint(jax.random.fold_in(own, 2), (rows, 1), 0, top)
    return jnp.take_along_axis(grid, (jnp.arange(top)[None, :] + offset_by) % top, axis=1)


def portions_of(count, total, reach, skew, full):
    loads = [(1 << 20) // math.isqrt(rank ** skew) + 1 for rank in range(1, count + 1)]
    largest = reach if full else min(reach, max(-(-total // count), total * loads[0] // sum(loads)))
    least = 1 if total - largest >= count - 1 else 0
    given, rest = [largest] + [least] * (count - 1), total - largest - least * (count - 1)
    while rest > 0:
        movable = [i for i in range(1, count) if given[i] < largest] or [i for i in range(1, count) if given[i] < reach]
        pool, left = sum([loads[i] for i in movable]), rest
        for i in movable:
            more = min(reach - given[i], max(1, left * loads[i] // pool), rest)
            given[i] = given[i] + more
            rest = rest - more
    return np.array(given)


def noise(own_key, dims, width, bound, cuts=(), kind=jnp.bfloat16):
    result = jax.random.normal(own_key, dims, jnp.float32) * width
    if len(cuts) > 0:
        result = level_of(own_key, dims, cuts, -0.22, 0.18) * result
    return jnp.clip(result, min=-bound, max=bound).astype(kind)


def setup_inputs(seed: int = 0) -> dict:
    keys = jax.random.split(jax.random.key(seed), 6)
    coords = draw_coords(jax.random.fold_in(keys[5], 71), 0)
    panel = noise(keys[1], (NPTS, SKETCH), 1.0, 6.0, ((0, 128),))
    mixing = noise(keys[2], (SKETCH, RANK), SKETCH ** -0.5, 0.5, (), jnp.float32)
    owners_keys = jax.random.split(jax.random.fold_in(keys[3], 1), NPAIRS // PAIRS_DEV)
    owners_turns = jax.random.permutation(jax.random.fold_in(keys[3], 3), NPAIRS // PAIRS_DEV)
    owners = jax.vmap(lambda own, number: deal_out(jax.random.fold_in(keys[3], 2), own, number, PAIRS_DEV, DEVICES, 1, CAP, 2))(owners_keys, owners_turns).reshape((NPAIRS, 1))
    leaf_picks = plant(jax.random.randint(keys[4], (NPAIRS, 2), 0, PT_DEV // LEAF), jax.random.fold_in(keys[4], 1), 0, (PT_DEV // LEAF) - 1).astype(jnp.int32)
    return {"coords": coords, "panel": panel, "mixing": mixing, "owners": owners, "leaf_picks": leaf_picks}


epsilon = 1e-06

def kernel_tile(left, right):
    highest = lax.Precision.HIGHEST
    left_sq = lax.optimization_barrier(jnp.sum(left * left, axis=0))
    right_sq = lax.optimization_barrier(jnp.sum(right * right, axis=0))
    inner_prod = jnp.einsum('dn,dm->nm', left, right, precision=highest)
    squared = left_sq[:, None] + right_sq[None, :] - 2.0 * inner_prod
    return jnp.exp(squared * (-2.0 / left.shape[0])).astype(jnp.bfloat16)

def make_bases(sketch_rows, mixing):
    highest = lax.Precision.HIGHEST
    narrow = jnp.einsum('lps,sr->lpr', sketch_rows, mixing, precision=highest)
    gram = jnp.einsum('lpr,lpq->lrq', narrow, narrow, precision=highest)
    scale = jnp.sqrt(lax.optimization_barrier(jnp.sum(gram * gram, axis=(1, 2))) + epsilon)
    iterate = gram / scale[:, None, None]
    ident = jnp.broadcast_to(jnp.eye(gram.shape[-1], dtype=gram.dtype), gram.shape)
    root = ident
    for sweep in range(NSWEEPS):
        factor = 1.5 * ident - 0.5 * jnp.einsum('lab,lbc->lac', root, iterate, precision=highest)
        iterate = jnp.einsum('lab,lbc->lac', iterate, factor, precision=highest)
        root = jnp.einsum('lab,lbc->lac', factor, root, precision=highest)
    basis = jnp.einsum('lpr,lrq->lpq', narrow, root, precision=highest) / jnp.sqrt(scale)[:, None, None]
    return basis.astype(jnp.bfloat16)

def reference(coords, panel, mixing, owners, leaf_picks):
    points = coords
    step_rows = math.gcd(NPTS, 512)
    blocks = points.reshape(DIM, NPTS // step_rows, step_rows).transpose(1, 0, 2)

    def one_block(block):
        return jnp.dot(kernel_tile(block, points), panel, preferred_element_type=jnp.float32)
    sketch = lax.map(one_block, blocks).reshape(NPTS, SKETCH)
    bases = make_bases(sketch.reshape(NLEAVES, LEAF, SKETCH), mixing)
    flat_bases = bases.reshape(NLEAVES, LEAF * RANK)
    pair_ids = jnp.arange(NPAIRS, dtype=jnp.int32)
    near = pair_ids // PAIRS_DEV * LEAVES_DEV + leaf_picks[:, 0]
    far = owners[:, 0] * LEAVES_DEV + leaf_picks[:, 1]
    group = math.gcd(NPAIRS, 64)

    def slice_leaf(offset):
        return lax.dynamic_slice_in_dim(points, (offset * LEAF).astype(jnp.int32), LEAF, 1)

    def couple(items):
        near_ids, far_ids = items
        near_pts = jax.vmap(slice_leaf)(near_ids)
        far_pts = jax.vmap(slice_leaf)(far_ids)
        kernels = jax.vmap(kernel_tile)(near_pts, far_pts)
        left = bases[near_ids].astype(jnp.float32)
        right = bases[far_ids].astype(jnp.float32)
        middle = jnp.einsum('gab,gbr->gar', kernels.astype(jnp.float32), right).astype(jnp.bfloat16)
        blocks_out = jnp.einsum('gar,gaq->grq', left, middle.astype(jnp.float32))
        return blocks_out.reshape(group, RANK * RANK)
    couplings = lax.map(couple, (near.reshape(-1, group), far.reshape(-1, group)))
    return (flat_bases, couplings.reshape(NPAIRS, RANK * RANK))
```

```python
import functools
import math

import jax
import jax.numpy as jnp
from jax import lax
from jax.experimental import pallas as pl
from jax.experimental.pallas import tpu as pltpu
from jax.sharding import PartitionSpec as P

MESH = pl.DeviceIdType.MESH
HIGHEST = lax.Precision.HIGHEST
f32, bf16 = jnp.float32, jnp.bfloat16

LEAF = 256
RANK = 64
NSWEEPS = 6
EPSILON = 1e-06
OWN = 512
UNIT = 128
UNITS = 4
PAIRS = 64
GROUP = 8
LINES = 32
SIDE = 4
CHUNK = 4096
PART_UNITS = (2, 1, 1)
PART_ROWS = tuple(RANK * u for u in PART_UNITS)
PART_BASE = (0, 128 * SIDE**3, 192 * SIDE**3)
CORE_ROWS = 256 * SIDE**3


def dot(a, b, dims, precision=None):
    return lax.dot_general(
        a, b, (dims, ((), ())), precision=precision, preferred_element_type=f32
    )


def pick3(k, a, b, c):
    return jnp.where(k == 0, a, jnp.where(k == 1, b, c))


def split3(v):
    hi = v.astype(bf16)
    rest = v - hi.astype(f32)
    mid = rest.astype(bf16)
    lo = (rest - mid.astype(f32)).astype(bf16)
    return hi, mid, lo


def features(x, column):
    n = x.shape[1]
    a = x * math.sqrt(4.0 * math.log2(math.e) / x.shape[0])
    h = -0.5 * jnp.sum(a * a, axis=0, keepdims=True)
    hi, mid, lo = split3(a)
    parts = [jnp.broadcast_to(v.astype(f32), (16, n)) for v in split3(h)]
    line = lax.broadcasted_iota(jnp.int32, (16, n), 0)
    at = 0 if column else 3
    extra = jnp.where(line < 6, 1.0, 0.0)
    for k in range(3):
        extra = jnp.where(line == at + k, parts[k], extra)
    extra = extra.astype(bf16)
    zero = jnp.zeros((16, n), bf16)
    if column:
        stack = [hi, hi, mid, mid, hi, lo, extra, zero]
    else:
        stack = [hi, mid, hi, mid, lo, hi, extra, zero]
    return jnp.concatenate(stack, axis=0)


class Place:
    def __init__(self):
        row, col = lax.axis_index("row"), lax.axis_index("col")
        self.core = lax.rem(row, 2)
        self.z = lax.div(row, 2)
        self.x = lax.div(col, SIDE)
        self.y = lax.rem(col, SIDE)
        self.index = row * SIDE * SIDE + col

    def sibling(self):
        return (self.z * 2 + 1 - self.core, self.x * SIDE + self.y)

    def neighbour(self, axis, step):
        x = lax.rem(self.x + jnp.where(axis == 0, step, 0), SIDE)
        y = lax.rem(self.y + jnp.where(axis == 1, step, 0), SIDE)
        z = lax.rem(self.z + jnp.where(axis == 2, step, 0), SIDE)
        return (z * 2 + self.core, x * SIDE + y)

    def along(self, turn):
        c = (self.x, self.y, self.z)
        return [pick3(turn, c[s], c[(s + 1) % 3], c[(s + 2) % 3]) for s in range(3)]


class Gather:
    def __init__(self, place, buf, send, recv, sib_send, sib_recv):
        self.place, self.buf = place, buf
        self.send, self.recv = send, recv
        self.sib_send, self.sib_recv = sib_send, sib_recv

    def turn(self, part):
        return lax.rem(part + self.place.core, 3)

    def start_row(self, part, slot):
        return self.place.core * CORE_ROWS + PART_BASE[part] + slot * PART_ROWS[part]

    def chunk_slot(self, part, stage, v):
        u = self.place.along(self.turn(part))
        if stage == 0:
            return u[2] * 16 + u[1] * 4 + v
        if stage == 1:
            return u[2] * 16 + v * 4
        return v * 16

    def hop(self, part, stage, hop, way):
        turn = self.turn(part)
        v = self.place.along(turn)[stage]
        rows = SIDE**stage * PART_ROWS[part]
        if hop == 0:
            start = self.start_row(part, self.chunk_slot(part, stage, v))
        else:
            from_v = lax.rem(v + (SIDE - 1 if way == 0 else 1), SIDE)
            rows //= 2
            start = self.start_row(part, self.chunk_slot(part, stage, from_v)) + way * rows
        ref = self.buf.at[pl.ds(lax.div(start, LINES), rows // LINES)]
        k = hop * 2 + way
        return pltpu.make_async_remote_copy(
            src_ref=ref,
            dst_ref=ref,
            send_sem=self.send.at[part, stage, k],
            recv_sem=self.recv.at[part, stage, k],
            device_id=self.place.neighbour(lax.rem(turn + stage, 3), 1 if way == 0 else SIDE - 1),
            device_id_type=MESH,
        )

    def side(self, part, piece):
        u2 = self.place.along(self.turn(part))[2]
        plane = lax.rem(u2 + (0, 1, 3, 2)[piece], SIDE)
        start = self.start_row(part, plane * 16)
        ref = self.buf.at[pl.ds(lax.div(start, LINES), 16 * PART_ROWS[part] // LINES)]
        return pltpu.make_async_remote_copy(
            src_ref=ref,
            dst_ref=ref,
            send_sem=self.sib_send.at[part, piece],
            recv_sem=self.sib_recv.at[part, piece],
            device_id=self.place.sibling(),
            device_id_type=MESH,
        )

    def hop_start(self, stage, hop):
        for part in range(3):
            for way in range(2):
                self.hop(part, stage, hop, way).start()

    def hop_wait(self, stage, hop):
        for part in range(3):
            for way in range(2):
                self.hop(part, stage, hop, way).wait_recv()

    def side_start(self, piece):
        for part in range(3):
            self.side(part, piece).start()

    def side_wait(self, piece):
        for part in range(3):
            self.side(part, piece).wait_recv()

    def own_rows(self):
        rows = []
        for part in range(3):
            u = self.place.along(self.turn(part))
            start = self.start_row(part, u[2] * 16 + u[1] * 4 + u[0])
            for unit in range(PART_UNITS[part]):
                rows.append(lax.div(start + unit * RANK, LINES))
        return rows

    def finish_sends(self):
        for part in range(3):
            for stage in range(3):
                for hop in range(2):
                    for way in range(2):
                        self.hop(part, stage, hop, way).wait_send()
            for piece in range(4):
                self.side(part, piece).wait_send()


def inverse_root(gram0, gram1):
    scales = [jnp.sqrt(jnp.sum(g * g) + EPSILON) for g in (gram0, gram1)]
    zero = jnp.zeros((RANK, RANK), f32)
    iterate = jnp.concatenate(
        [
            jnp.concatenate([gram0 / scales[0], zero], axis=1),
            jnp.concatenate([zero, gram1 / scales[1]], axis=1),
        ],
        axis=0,
    )
    shape = (2 * RANK, 2 * RANK)
    ident = jnp.where(
        lax.broadcasted_iota(jnp.int32, shape, 0) == lax.broadcasted_iota(jnp.int32, shape, 1),
        1.0,
        0.0,
    )
    root = ident
    for sweep in range(NSWEEPS):
        product = iterate if sweep == 0 else dot(root, iterate, ((1,), (0,)), HIGHEST)
        factor = 1.5 * ident - 0.5 * product
        if sweep < NSWEEPS - 1:
            iterate = dot(iterate, factor, ((1,), (0,)), HIGHEST)
        root = factor if sweep == 0 else dot(factor, root, ((1,), (0,)), HIGHEST)
    return root, scales


def kernel(
    coords, panel, mixing, rows_of, bases_out, coup_out,
    f_ref, q_ref, b_ref, g_ref, gt_ref, l_ref, bs_ref, sc_ref, sct_ref, st_ref,
    q_send, q_recv, q_sib_send, q_sib_recv, b_send, b_recv, b_sib_send, b_sib_recv,
):
    place = Place()
    gather_q = Gather(place, q_ref, q_send, q_recv, q_sib_send, q_sib_recv)
    gather_b = Gather(place, b_ref, b_send, b_recv, b_sib_send, b_sib_recv)

    barrier = pltpu.get_barrier_semaphore()
    peers = [place.neighbour(axis, step) for axis in range(3) for step in (1, SIDE - 1)]
    peers.append(place.sibling())
    for peer in peers:
        pl.semaphore_signal(barrier, inc=1, device_id=peer, device_id_type=MESH)

    vectors = dot(mixing[...], panel[...].astype(f32), ((0,), (1,)), HIGHEST).astype(bf16)
    for unit, row in enumerate(gather_q.own_rows()):
        for n in range(2):
            q_ref[row + n] = vectors[LINES * n : LINES * (n + 1), unit * UNIT : (unit + 1) * UNIT]
    pl.semaphore_wait(barrier, len(peers))

    gather_q.hop_start(0, 0)
    own = coords[:, pl.ds(pl.multiple_of(place.index * OWN, OWN), OWN)]
    own_features = features(own, False)
    g_ref[...] = own_features
    for leaf in range(2):
        gt_ref[leaf] = own_features[:, leaf * LEAF : (leaf + 1) * LEAF].T
    for stage in range(2):
        gather_q.hop_wait(stage, 0)
        gather_q.hop_start(stage, 1)
        gather_q.hop_wait(stage, 1)
        gather_q.hop_start(stage + 1, 0)
    gather_q.side_start(0)

    def sketch_step(i, total):
        @pl.when(i == 2)
        def _():
            gather_q.side_wait(0)

        @pl.when(i == 4)
        def _():
            gather_q.hop_wait(2, 0)
            gather_q.hop_start(2, 1)
            gather_q.side_start(1)
            gather_q.side_start(2)

        @pl.when(i == 6)
        def _():
            gather_q.side_wait(1)

        @pl.when(i == 10)
        def _():
            gather_q.side_wait(2)

        @pl.when(i == 12)
        def _():
            gather_q.hop_wait(2, 1)
            gather_q.side_start(3)

        @pl.when(i == 14)
        def _():
            gather_q.side_wait(3)

        quarter = lax.div(i, 4)
        step = quarter + jnp.where(quarter == 2, 1, 0) - jnp.where(quarter == 3, 1, 0)
        other = lax.rem(lax.div(i, 2), 2)
        second = lax.rem(i, 2)
        core = lax.rem(place.core + other, 2)
        device_at, row_at = [], []
        for part in range(3):
            turn = lax.rem(part + core, 3)
            w = [pick3(turn, *((4, 1, 32) * 2)[s : s + 3]) for s in range(3)]
            u2 = lax.rem(place.along(turn)[2] + step, SIDE)
            device_at.append((core * 16 + u2 * w[2], w[1], w[0]))
            row_at.append(core * CORE_ROWS + PART_BASE[part] + u2 * 16 * PART_ROWS[part])
        pieces, vectors, places = [], [], []
        for n in range(CHUNK // UNIT):
            slot, unit = n // 2, n % 2
            base, w1, w0 = device_at[0]
            point0 = (base + (slot // 4) * w1 + (slot % 4) * w0) * OWN + unit * UNIT
            row0 = row_at[0] + slot * PART_ROWS[0] + unit * RANK
            slot, part = n % 16, 1 + n // 16
            base, w1, w0 = device_at[part]
            point1 = (base + (slot // 4) * w1 + (slot % 4) * w0) * OWN + (part + 1) * UNIT
            row1 = row_at[part] + slot * PART_ROWS[part]
            point = pl.multiple_of(jnp.where(second == 0, point0, point1), UNIT)
            row = lax.div(jnp.where(second == 0, row0, row1), LINES)
            places.append(point)
            pieces.append(coords[:, pl.ds(point, UNIT)])
            vectors.append(jnp.concatenate([q_ref[row], q_ref[row + 1]], axis=0))
        columns = features(jnp.concatenate(pieces, axis=1), True).T
        for n, point in enumerate(places):
            f_ref[lax.div(point, UNIT)] = columns[n * UNIT : (n + 1) * UNIT, :]
        tile = jnp.exp2(dot(columns, g_ref[...], ((1,), (0,)))).astype(bf16)
        return total + dot(jnp.concatenate(vectors, axis=1), tile, ((1,), (0,)))

    narrow = lax.fori_loop(0, 16, sketch_step, jnp.zeros((RANK, OWN), f32))

    grams = [dot(n, n, ((1,), (1,)), HIGHEST) for n in (narrow[:, :LEAF], narrow[:, LEAF:])]
    root, scales = inverse_root(*grams)
    stacked = jnp.concatenate([narrow[:, :LEAF], narrow[:, LEAF:]], axis=0)
    left = lax.broadcasted_iota(jnp.int32, (1, 2 * RANK), 1) < RANK
    scale = jnp.sqrt(jnp.where(left, scales[0], scales[1]))
    rounded = (dot(stacked, root, ((0,), (0,)), HIGHEST) / scale).astype(bf16)
    for unit, row in enumerate(gather_b.own_rows()):
        for n in range(2):
            at = unit * RANK + LINES * n
            b_ref[row + n] = rounded[at : at + LINES, :]
    gather_b.hop_start(0, 0)

    packed = rounded.astype(f32)
    sc_ref[...] = packed
    flipped = packed.T
    for side in range(2):
        sct_ref[128 * side : 128 * (side + 1), :] = flipped[:, 128 * side : 128 * (side + 1)]
    even, odd = sc_ref[pl.ds(0, 128, stride=2), :], sc_ref[pl.ds(1, 128, stride=2), :]
    bases_out[0] = jnp.where(left, even, pltpu.roll(odd, RANK, 1)).astype(bf16)
    bases_out[1] = jnp.where(left, pltpu.roll(even, RANK, 1), odd).astype(bf16)
    half = RANK // 2
    for leaf in range(2):
        for odd_one in range(2):
            at = odd_one * half
            for side in range(2):
                first = 128 * side + leaf * RANK + odd_one
                bs_ref[leaf, at : at + half, 128 * side : 128 * (side + 1)] = sct_ref[
                    pl.ds(first, half, stride=2), :
                ].astype(bf16)

    def near_step(g, carry):
        for hop in range(4):

            @pl.when(g == hop + 1)
            def _(hop=hop):
                gather_b.hop_wait(hop // 2, hop % 2)
                gather_b.hop_start((hop + 1) // 2, (hop + 1) % 2)
                if hop == 3:
                    gather_b.side_start(0)

        for n in range(GROUP):
            k = g * GROUP + n
            near, far = rows_of[0, k], rows_of[1, k]
            near_rows = gt_ref[near]
            far_rows = jnp.concatenate([f_ref[far], f_ref[far + 1]], axis=0)
            tile = jnp.exp2(dot(near_rows, far_rows, ((1,), (1,)))).astype(bf16)
            l_ref[k] = dot(bs_ref[near], tile, ((1,), (0,))).astype(bf16)
        return carry

    lax.fori_loop(0, PAIRS // GROUP, near_step, 0)

    gather_b.hop_wait(2, 0)
    gather_b.hop_start(2, 1)
    gather_b.side_start(1)
    gather_b.side_start(2)
    gather_b.hop_wait(2, 1)
    gather_b.side_start(3)
    for piece in range(4):
        gather_b.side_wait(piece)

    def far_step(g, carry):
        for pair in range(GROUP):
            k = g * GROUP + pair
            blocks = []
            for part in range(3):
                row = rows_of[2 + part, k]
                for n in range(PART_ROWS[part] // LINES):
                    blocks.append(b_ref[row + n])
            both = dot(
                l_ref[k],
                jnp.concatenate(blocks, axis=0),
                ((1,), (0,)),
            )
            even, odd = both[:half, :], both[half:, :]
            first = jnp.where(left, even, pltpu.roll(odd, RANK, 1))
            second = jnp.where(left, pltpu.roll(even, RANK, 1), odd)
            pick = rows_of[5, k].astype(f32)
            st_ref[pair * half : (pair + 1) * half, :] = first * (1.0 - pick) + second * pick
        rows = pl.ds(pl.multiple_of(g * GROUP, GROUP), GROUP)
        for i in range(half):
            coup_out[rows, 128 * i : 128 * (i + 1)] = st_ref[pl.ds(i, GROUP, stride=half), :]
        return carry

    lax.fori_loop(0, PAIRS // GROUP, far_step, 0)
    gather_q.finish_sends()
    gather_b.finish_sends()


def pair_rows(owner, near, pick):
    line, col = owner // 16, owner % 16
    core, z, x, y = line % 2, line // 2, col // SIDE, col % SIDE
    slots = [z * 16 + y * 4 + x, x * 16 + z * 4 + y, y * 16 + x * 4 + z]
    rows = [near, (owner * 2 + pick) * 2]
    for part in range(3):
        slot = jnp.where(core == 0, slots[part], slots[(part + 1) % 3])
        rows.append((core * CORE_ROWS + PART_BASE[part] + slot * PART_ROWS[part]) // LINES)
    return jnp.stack(rows + [pick])


def per_device(coords, panel, mixing, owners, leaf_picks):
    vmem = pl.BlockSpec(memory_space=pltpu.VMEM)
    smem = pl.BlockSpec(memory_space=pltpu.SMEM)
    sems = pltpu.SemaphoreType.DMA
    points = coords.shape[1]
    bases, couplings = pl.pallas_call(
        kernel,
        out_shape=(
            jax.ShapeDtypeStruct((2, 128, 128), bf16),
            jax.ShapeDtypeStruct((PAIRS, RANK * RANK), f32),
        ),
        in_specs=[vmem, vmem, vmem, smem],
        out_specs=(vmem, vmem),
        scratch_shapes=[
            pltpu.VMEM((points // UNIT, UNIT, 128), bf16),
            pltpu.VMEM((2 * CORE_ROWS // LINES, LINES, 128), bf16),
            pltpu.VMEM((2 * CORE_ROWS // LINES, LINES, 128), bf16),
            pltpu.VMEM((128, OWN), bf16),
            pltpu.VMEM((2, LEAF, 128), bf16),
            pltpu.VMEM((PAIRS, RANK, LEAF), bf16),
            pltpu.VMEM((2, RANK, LEAF), bf16),
            pltpu.VMEM((LEAF, 128), f32),
            pltpu.VMEM((2 * 128, 128), f32),
            pltpu.VMEM((GROUP * RANK // 2, 128), f32),
            sems((3, 3, 4)),
            sems((3, 3, 4)),
            sems((3, 4)),
            sems((3, 4)),
            sems((3, 3, 4)),
            sems((3, 3, 4)),
            sems((3, 4)),
            sems((3, 4)),
        ],
        compiler_params=pltpu.CompilerParams(
            collective_id=0, has_side_effects=True, vmem_limit_bytes=60 * 2**20
        ),
    )(coords, panel, mixing, pair_rows(owners[:, 0], leaf_picks[:, 0], leaf_picks[:, 1]))
    return bases.reshape(2, LEAF * RANK), couplings


def solution(mesh):
    return jax.shard_map(
        per_device,
        mesh=mesh,
        in_specs=(
            P(),
            P(("row", "col"), None),
            P(),
            P(("row", "col"), None),
            P(("row", "col"), None),
        ),
        out_specs=(P(("row", "col"), None), P(("row", "col"), None)),
        check_vma=False,
    )
```

```python
import functools
import math

import jax
import jax.numpy as jnp
from jax import lax
from jax.experimental import pallas as pl
from jax.experimental.pallas import tpu as pltpu
from jax.sharding import PartitionSpec as P

MESH = pl.DeviceIdType.MESH
HIGHEST = lax.Precision.HIGHEST
f32, bf16 = jnp.float32, jnp.bfloat16

LEAF = 256
RANK = 64
NSWEEPS = 6
EPSILON = 1e-06
OWN = 512
UNIT = 128
UNITS = 4
PAIRS = 64
GROUP = 8
LINES = 32
SIDE = 4
CHUNK = 4096
PART_UNITS = (2, 1, 1)
PART_ROWS = tuple(RANK * u for u in PART_UNITS)
PART_BASE = (0, 128 * SIDE**3, 192 * SIDE**3)
CORE_ROWS = 256 * SIDE**3


def dot(a, b, dims, precision=None):
    return lax.dot_general(
        a, b, (dims, ((), ())), precision=precision, preferred_element_type=f32
    )


def pick3(k, a, b, c):
    return jnp.where(k == 0, a, jnp.where(k == 1, b, c))


def split3(v):
    hi = v.astype(bf16)
    rest = v - hi.astype(f32)
    mid = rest.astype(bf16)
    lo = (rest - mid.astype(f32)).astype(bf16)
    return hi, mid, lo


def features(x, column):
    n = x.shape[1]
    a = x * math.sqrt(4.0 * math.log2(math.e) / x.shape[0])
    h = -0.5 * jnp.sum(a * a, axis=0, keepdims=True)
    hi, mid, lo = split3(a)
    parts = [jnp.broadcast_to(v.astype(f32), (16, n)) for v in split3(h)]
    line = lax.broadcasted_iota(jnp.int32, (16, n), 0)
    at = 0 if column else 3
    extra = jnp.where(line < 6, 1.0, 0.0)
    for k in range(3):
        extra = jnp.where(line == at + k, parts[k], extra)
    extra = extra.astype(bf16)
    zero = jnp.zeros((16, n), bf16)
    if column:
        stack = [hi, hi, mid, mid, hi, lo, extra, zero]
    else:
        stack = [hi, mid, hi, mid, lo, hi, extra, zero]
    return jnp.concatenate(stack, axis=0)


class Place:
    def __init__(self):
        row, col = lax.axis_index("row"), lax.axis_index("col")
        self.core = lax.rem(row, 2)
        self.z = lax.div(row, 2)
        self.x = lax.div(col, SIDE)
        self.y = lax.rem(col, SIDE)
        self.index = row * SIDE * SIDE + col

    def sibling(self):
        return (self.z * 2 + 1 - self.core, self.x * SIDE + self.y)

    def neighbour(self, axis, step):
        x = lax.rem(self.x + jnp.where(axis == 0, step, 0), SIDE)
        y = lax.rem(self.y + jnp.where(axis == 1, step, 0), SIDE)
        z = lax.rem(self.z + jnp.where(axis == 2, step, 0), SIDE)
        return (z * 2 + self.core, x * SIDE + y)

    def along(self, turn):
        c = (self.x, self.y, self.z)
        return [pick3(turn, c[s], c[(s + 1) % 3], c[(s + 2) % 3]) for s in range(3)]


class Gather:
    def __init__(self, place, buf, send, recv, sib_send, sib_recv):
        self.place, self.buf = place, buf
        self.send, self.recv = send, recv
        self.sib_send, self.sib_recv = sib_send, sib_recv

    def turn(self, part):
        return lax.rem(part + self.place.core, 3)

    def start_row(self, part, slot):
        return self.place.core * CORE_ROWS + PART_BASE[part] + slot * PART_ROWS[part]

    def chunk_slot(self, part, stage, v):
        u = self.place.along(self.turn(part))
        if stage == 0:
            return u[2] * 16 + u[1] * 4 + v
        if stage == 1:
            return u[2] * 16 + v * 4
        return v * 16

    def copy(self, part, stage, v, first, count, step, sem):
        turn = self.turn(part)
        start = self.start_row(part, self.chunk_slot(part, stage, v)) + first
        ref = self.buf.at[pl.ds(lax.div(start, LINES), count // LINES)]
        return pltpu.make_async_remote_copy(
            src_ref=ref,
            dst_ref=ref,
            send_sem=self.send.at[part, sem],
            recv_sem=self.recv.at[part, sem],
            device_id=self.place.neighbour(lax.rem(turn + stage, 3), step),
            device_id_type=MESH,
        )

    def copies(self, part, what):
        stage = min(what, 2)
        v = self.place.along(self.turn(part))[stage]
        rows = SIDE**stage * PART_ROWS[part]
        if what < 2:
            return [self.copy(part, stage, v, 0, rows, s, 3 * what + s - 1) for s in (1, 2, 3)]
        half = rows // 2
        result = []
        for way, step in enumerate((1, SIDE - 1)):
            first = half * (way if what != 3 else 1 - way)
            at = v if what < 4 else lax.rem(v + SIDE - step, SIDE)
            result.append(self.copy(part, stage, at, first, half, step, 2 * what + 2 + way))
        return result

    def side(self, part, piece):
        u2 = self.place.along(self.turn(part))[2]
        plane = lax.rem(u2 + (0, 1, 3, 2)[piece], SIDE)
        start = self.start_row(part, plane * 16)
        ref = self.buf.at[pl.ds(lax.div(start, LINES), 16 * PART_ROWS[part] // LINES)]
        return pltpu.make_async_remote_copy(
            src_ref=ref,
            dst_ref=ref,
            send_sem=self.sib_send.at[part, piece],
            recv_sem=self.sib_recv.at[part, piece],
            device_id=self.place.sibling(),
            device_id_type=MESH,
        )

    def start(self, what):
        for part in range(3):
            for copy in self.copies(part, what):
                copy.start()

    def wait(self, what):
        for part in range(3):
            for copy in self.copies(part, what):
                copy.wait_recv()

    def side_start(self, piece):
        for part in range(3):
            self.side(part, piece).start()

    def side_wait(self, piece):
        for part in range(3):
            self.side(part, piece).wait_recv()

    def own_rows(self):
        rows = []
        for part in range(3):
            u = self.place.along(self.turn(part))
            start = self.start_row(part, u[2] * 16 + u[1] * 4 + u[0])
            for unit in range(PART_UNITS[part]):
                rows.append(lax.div(start + unit * RANK, LINES))
        return rows

    def finish_sends(self):
        for part in range(3):
            for what in range(5):
                for copy in self.copies(part, what):
                    copy.wait_send()
            for piece in range(4):
                self.side(part, piece).wait_send()


def inverse_root(gram0, gram1):
    scales = [jnp.sqrt(jnp.sum(g * g) + EPSILON) for g in (gram0, gram1)]
    zero = jnp.zeros((RANK, RANK), f32)
    iterate = jnp.concatenate(
        [
            jnp.concatenate([gram0 / scales[0], zero], axis=1),
            jnp.concatenate([zero, gram1 / scales[1]], axis=1),
        ],
        axis=0,
    )
    shape = (2 * RANK, 2 * RANK)
    ident = jnp.where(
        lax.broadcasted_iota(jnp.int32, shape, 0) == lax.broadcasted_iota(jnp.int32, shape, 1),
        1.0,
        0.0,
    )
    root = ident
    for sweep in range(NSWEEPS):
        product = iterate if sweep == 0 else dot(root, iterate, ((1,), (0,)), HIGHEST)
        factor = 1.5 * ident - 0.5 * product
        if sweep < NSWEEPS - 1:
            iterate = dot(iterate, factor, ((1,), (0,)), HIGHEST)
        root = factor if sweep == 0 else dot(factor, root, ((1,), (0,)), HIGHEST)
    return root, scales


def kernel(
    coords, panel, mixing, owners, picks, bases_out, coup_out,
    x_ref, q_ref, b_ref, k_ref, g_ref, gt_ref, l_ref, bs_ref, sc_ref, sct_ref, st_ref,
    q_send, q_recv, q_sib_send, q_sib_recv, b_send, b_recv, b_sib_send, b_sib_recv,
):
    place = Place()
    gather_q = Gather(place, q_ref, q_send, q_recv, q_sib_send, q_sib_recv)
    gather_b = Gather(place, b_ref, b_send, b_recv, b_sib_send, b_sib_recv)

    barrier = pltpu.get_barrier_semaphore()
    peers = [place.neighbour(axis, step) for axis in range(3) for step in (1, 2, 3)]
    peers.append(place.sibling())
    for peer in peers:
        pl.semaphore_signal(barrier, inc=1, device_id=peer, device_id_type=MESH)

    vectors = dot(mixing[...], panel[...].astype(f32), ((1,), (1,)), HIGHEST).astype(bf16)
    for unit, row in enumerate(gather_q.own_rows()):
        for n in range(2):
            q_ref[row + n] = vectors[LINES * n : LINES * (n + 1), unit * UNIT : (unit + 1) * UNIT]
    pl.semaphore_wait(barrier, len(peers))

    gather_q.start(0)
    own = coords[:, pl.ds(pl.multiple_of(place.index * OWN, OWN), OWN)]
    own_features = features(own, False)
    g_ref[...] = own_features
    for leaf in range(2):
        gt_ref[leaf] = own_features[:, leaf * LEAF : (leaf + 1) * LEAF].T
    for unit in range(coords.shape[1] // UNIT):
        x_ref[unit] = coords[:, unit * UNIT : (unit + 1) * UNIT]

    def pair_step(g, carry):
        @pl.when(g == 3)
        def _():
            gather_q.wait(0)
            gather_q.start(1)

        far = []
        for n in range(GROUP):
            entry = (owners[0, g * GROUP + n] * 2 + picks[1, g * GROUP + n]) * 2
            far += [x_ref[entry], x_ref[entry + 1]]
        far = features(jnp.concatenate(far, axis=1), True)
        for n in range(GROUP):
            near_rows = gt_ref[picks[0, g * GROUP + n]]
            exponent = dot(near_rows, far[:, n * LEAF : (n + 1) * LEAF], ((1,), (0,)))
            k_ref[g * GROUP + n] = jnp.exp2(exponent).astype(bf16)
        return carry

    lax.fori_loop(0, PAIRS // GROUP, pair_step, 0)
    gather_q.wait(1)
    gather_q.start(2)
    gather_q.start(3)
    gather_q.side_start(0)

    def sketch_step(i, total):
        @pl.when(i == 2)
        def _():
            gather_q.side_wait(0)

        @pl.when(i == 4)
        def _():
            gather_q.wait(2)
            gather_q.start(4)
            gather_q.wait(3)
            gather_q.side_start(1)
            gather_q.side_start(2)

        @pl.when(i == 6)
        def _():
            gather_q.side_wait(1)

        @pl.when(i == 10)
        def _():
            gather_q.side_wait(2)

        @pl.when(i == 12)
        def _():
            gather_q.wait(4)
            gather_q.side_start(3)

        @pl.when(i == 14)
        def _():
            gather_q.side_wait(3)

        quarter = lax.div(i, 4)
        step = quarter + jnp.where(quarter == 2, 1, 0) - jnp.where(quarter == 3, 1, 0)
        other = lax.rem(lax.div(i, 2), 2)
        second = lax.rem(i, 2)
        core = lax.rem(place.core + other, 2)
        device_at, row_at = [], []
        for part in range(3):
            turn = lax.rem(part + core, 3)
            w = [pick3(turn, *((4, 1, 32) * 2)[s : s + 3]) for s in range(3)]
            u2 = lax.rem(place.along(turn)[2] + step, SIDE)
            device_at.append((core * 16 + u2 * w[2], w[1], w[0]))
            row_at.append(core * CORE_ROWS + PART_BASE[part] + u2 * 16 * PART_ROWS[part])
        pieces, vectors = [], []
        for n in range(CHUNK // UNIT):
            slot, unit = n // 2, n % 2
            base, w1, w0 = device_at[0]
            point0 = (base + (slot // 4) * w1 + (slot % 4) * w0) * OWN + unit * UNIT
            row0 = row_at[0] + slot * PART_ROWS[0] + unit * RANK
            slot, part = n % 16, 1 + n // 16
            base, w1, w0 = device_at[part]
            point1 = (base + (slot // 4) * w1 + (slot % 4) * w0) * OWN + (part + 1) * UNIT
            row1 = row_at[part] + slot * PART_ROWS[part]
            point = jnp.where(second == 0, point0, point1)
            row = lax.div(jnp.where(second == 0, row0, row1), LINES)
            pieces.append(x_ref[lax.div(point, UNIT)])
            vectors.append(jnp.concatenate([q_ref[row], q_ref[row + 1]], axis=0))
        columns = features(jnp.concatenate(pieces, axis=1), True).T
        tile = jnp.exp2(dot(columns, g_ref[...], ((1,), (0,)))).astype(bf16)
        return total + dot(jnp.concatenate(vectors, axis=1), tile, ((1,), (0,)))

    narrow = lax.fori_loop(0, 16, sketch_step, jnp.zeros((RANK, OWN), f32))

    grams = [dot(n, n, ((1,), (1,)), HIGHEST) for n in (narrow[:, :LEAF], narrow[:, LEAF:])]
    root, scales = inverse_root(*grams)
    stacked = jnp.concatenate([narrow[:, :LEAF], narrow[:, LEAF:]], axis=0)
    left = lax.broadcasted_iota(jnp.int32, (1, 2 * RANK), 1) < RANK
    scale = jnp.sqrt(jnp.where(left, scales[0], scales[1]))
    rounded = (dot(stacked, root, ((0,), (0,)), HIGHEST) / scale).astype(bf16)
    for unit, row in enumerate(gather_b.own_rows()):
        for n in range(2):
            at = unit * RANK + LINES * n
            b_ref[row + n] = rounded[at : at + LINES, :]
    gather_b.start(0)

    packed = rounded.astype(f32)
    sc_ref[...] = packed
    flipped = packed.T
    for side in range(2):
        sct_ref[128 * side : 128 * (side + 1), :] = flipped[:, 128 * side : 128 * (side + 1)]
    even, odd = sc_ref[pl.ds(0, 128, stride=2), :], sc_ref[pl.ds(1, 128, stride=2), :]
    bases_out[0] = jnp.where(left, even, pltpu.roll(odd, RANK, 1)).astype(bf16)
    bases_out[1] = jnp.where(left, pltpu.roll(even, RANK, 1), odd).astype(bf16)
    half = RANK // 2
    for leaf in range(2):
        for odd_one in range(2):
            at = odd_one * half
            for side in range(2):
                first = 128 * side + leaf * RANK + odd_one
                bs_ref[leaf, at : at + half, 128 * side : 128 * (side + 1)] = sct_ref[
                    pl.ds(first, half, stride=2), :
                ].astype(bf16)

    def near_step(g, carry):
        for n in range(GROUP):
            k = g * GROUP + n
            l_ref[k] = dot(bs_ref[picks[0, k]], k_ref[k], ((1,), (0,))).astype(bf16)
        return carry

    lax.fori_loop(0, PAIRS // GROUP, near_step, 0)

    gather_b.wait(0)
    gather_b.start(1)
    gather_b.wait(1)
    gather_b.start(2)
    gather_b.start(3)
    gather_b.side_start(0)
    gather_b.wait(2)
    gather_b.start(4)
    gather_b.wait(3)
    gather_b.side_start(1)
    gather_b.side_start(2)
    gather_b.wait(4)
    gather_b.side_start(3)
    for piece in range(4):
        gather_b.side_wait(piece)

    def far_step(g, carry):
        for pair in range(GROUP):
            k = g * GROUP + pair
            line, col = lax.div(owners[0, k], 16), lax.rem(owners[0, k], 16)
            core, z = lax.rem(line, 2), lax.div(line, 2)
            x, y = lax.div(col, SIDE), lax.rem(col, SIDE)
            slots = [z * 16 + y * 4 + x, x * 16 + z * 4 + y, y * 16 + x * 4 + z]
            blocks = []
            for part in range(3):
                slot = slots[part] + core * (slots[(part + 1) % 3] - slots[part])
                row = core * (CORE_ROWS // LINES) + PART_BASE[part] // LINES + slot * (PART_ROWS[part] // LINES)
                for n in range(PART_ROWS[part] // LINES):
                    blocks.append(b_ref[row + n])
            both = dot(
                l_ref[k],
                jnp.concatenate(blocks, axis=0),
                ((1,), (0,)),
            )
            even, odd = both[:half, :], both[half:, :]
            first = jnp.where(left, even, pltpu.roll(odd, RANK, 1))
            second = jnp.where(left, pltpu.roll(even, RANK, 1), odd)
            pick = picks[1, k].astype(f32)
            st_ref[pair * half : (pair + 1) * half, :] = first * (1.0 - pick) + second * pick
        rows = pl.ds(pl.multiple_of(g * GROUP, GROUP), GROUP)
        for i in range(half):
            coup_out[rows, 128 * i : 128 * (i + 1)] = st_ref[pl.ds(i, GROUP, stride=half), :]
        return carry

    lax.fori_loop(0, PAIRS // GROUP, far_step, 0)
    gather_q.finish_sends()
    gather_b.finish_sends()


def per_device(coords, panel, mixing, owners, leaf_picks):
    vmem = pl.BlockSpec(memory_space=pltpu.VMEM)
    smem = pl.BlockSpec(memory_space=pltpu.SMEM)
    sems = pltpu.SemaphoreType.DMA
    points = coords.shape[1]
    bases, couplings = pl.pallas_call(
        kernel,
        out_shape=(
            jax.ShapeDtypeStruct((2, 128, 128), bf16),
            jax.ShapeDtypeStruct((PAIRS, RANK * RANK), f32),
        ),
        in_specs=[vmem, vmem, vmem, smem, smem],
        out_specs=(vmem, vmem),
        scratch_shapes=[
            pltpu.VMEM((points // UNIT, coords.shape[0], UNIT), f32),
            pltpu.VMEM((2 * CORE_ROWS // LINES, LINES, 128), bf16),
            pltpu.VMEM((2 * CORE_ROWS // LINES, LINES, 128), bf16),
            pltpu.VMEM((PAIRS, LEAF, LEAF), bf16),
            pltpu.VMEM((128, OWN), bf16),
            pltpu.VMEM((2, LEAF, 128), bf16),
            pltpu.VMEM((PAIRS, RANK, LEAF), bf16),
            pltpu.VMEM((2, RANK, LEAF), bf16),
            pltpu.VMEM((LEAF, 128), f32),
            pltpu.VMEM((2 * 128, 128), f32),
            pltpu.VMEM((GROUP * RANK // 2, 128), f32),
            sems((3, 12)),
            sems((3, 12)),
            sems((3, 4)),
            sems((3, 4)),
            sems((3, 12)),
            sems((3, 12)),
            sems((3, 4)),
            sems((3, 4)),
        ],
        compiler_params=pltpu.CompilerParams(
            collective_id=0, has_side_effects=True, vmem_limit_bytes=60 * 2**20
        ),
    )(coords, panel, mixing.T, owners.T, leaf_picks.T)
    return bases.reshape(2, LEAF * RANK), couplings


def solution(mesh):
    return jax.shard_map(
        per_device,
        mesh=mesh,
        in_specs=(
            P(),
            P(("row", "col"), None),
            P(),
            P(("row", "col"), None),
            P(("row", "col"), None),
        ),
        out_specs=(P(("row", "col"), None), P(("row", "col"), None)),
        check_vma=False,
    )
```

```python
import functools
import math

import jax
import jax.numpy as jnp
from jax import lax
from jax.experimental import pallas as pl
from jax.experimental.pallas import tpu as pltpu
from jax.sharding import PartitionSpec as P

MESH = pl.DeviceIdType.MESH
HIGHEST = lax.Precision.HIGHEST
f32, bf16 = jnp.float32, jnp.bfloat16

LEAF = 256
RANK = 64
NSWEEPS = 6
EPSILON = 1e-06
OWN = 512
UNIT = 128
UNITS = 4
PAIRS = 64
GROUP = 8
LINES = 32
SIDE = 4
CHUNK = 4096
EARLY = 3
INPUTS = 8
PART_UNITS = (2, 1, 1)
PART_ROWS = tuple(RANK * u for u in PART_UNITS)
PART_BASE = (0, 128 * SIDE**3, 192 * SIDE**3)
CORE_ROWS = 256 * SIDE**3


def dot(a, b, dims, precision=None):
    return lax.dot_general(
        a, b, (dims, ((), ())), precision=precision, preferred_element_type=f32
    )


def pick3(k, a, b, c):
    return jnp.where(k == 0, a, jnp.where(k == 1, b, c))


def split3(v):
    hi = v.astype(bf16)
    rest = v - hi.astype(f32)
    mid = rest.astype(bf16)
    lo = (rest - mid.astype(f32)).astype(bf16)
    return hi, mid, lo


def features(x, column):
    n = x.shape[1]
    a = x * math.sqrt(4.0 * math.log2(math.e) / x.shape[0])
    h = -0.5 * jnp.sum(a * a, axis=0, keepdims=True)
    hi, mid, lo = split3(a)
    parts = [jnp.broadcast_to(v.astype(f32), (16, n)) for v in split3(h)]
    line = lax.broadcasted_iota(jnp.int32, (16, n), 0)
    at = 0 if column else 3
    extra = jnp.where(line < 6, 1.0, 0.0)
    for k in range(3):
        extra = jnp.where(line == at + k, parts[k], extra)
    extra = extra.astype(bf16)
    zero = jnp.zeros((16, n), bf16)
    if column:
        stack = [hi, hi, mid, mid, hi, lo, extra, zero]
    else:
        stack = [hi, mid, hi, mid, lo, hi, extra, zero]
    return jnp.concatenate(stack, axis=0)


class Place:
    def __init__(self):
        row, col = lax.axis_index("row"), lax.axis_index("col")
        self.core = lax.rem(row, 2)
        self.z = lax.div(row, 2)
        self.x = lax.div(col, SIDE)
        self.y = lax.rem(col, SIDE)
        self.index = row * SIDE * SIDE + col

    def sibling(self):
        return (self.z * 2 + 1 - self.core, self.x * SIDE + self.y)

    def neighbour(self, axis, step):
        x = lax.rem(self.x + jnp.where(axis == 0, step, 0), SIDE)
        y = lax.rem(self.y + jnp.where(axis == 1, step, 0), SIDE)
        z = lax.rem(self.z + jnp.where(axis == 2, step, 0), SIDE)
        return (z * 2 + self.core, x * SIDE + y)

    def along(self, turn):
        c = (self.x, self.y, self.z)
        return [pick3(turn, c[s], c[(s + 1) % 3], c[(s + 2) % 3]) for s in range(3)]


class Gather:
    def __init__(self, place, buf, send, recv, sib_send, sib_recv):
        self.place, self.buf = place, buf
        self.send, self.recv = send, recv
        self.sib_send, self.sib_recv = sib_send, sib_recv

    def turn(self, part):
        return lax.rem(part + self.place.core, 3)

    def start_row(self, part, slot):
        return self.place.core * CORE_ROWS + PART_BASE[part] + slot * PART_ROWS[part]

    def ref(self, part, plane, group, slot, slots):
        first = lax.rem(plane, SIDE) * 16 + lax.rem(group, SIDE) * 4 + slot
        start = lax.div(self.start_row(part, first), LINES)
        return self.buf.at[pl.ds(start, slots * PART_ROWS[part] // LINES)]

    def copy(self, part, stage, ref, step, sem):
        return pltpu.make_async_remote_copy(
            src_ref=ref,
            dst_ref=ref,
            send_sem=self.send.at[part, sem],
            recv_sem=self.recv.at[part, sem],
            device_id=self.place.neighbour(lax.rem(self.turn(part) + stage, 3), step),
            device_id_type=MESH,
        )

    def first(self, stage):
        result = []
        for part in range(3):
            u = self.place.along(self.turn(part))
            ref = self.ref(part, u[2], u[1], u[0] if stage == 0 else 0, 1 if stage == 0 else 4)
            result += [self.copy(part, stage, ref, s, 3 * stage + s - 1) for s in (1, 2, 3)]
        return result

    def near_plane(self, r):
        result = []
        for part in range(3):
            u = self.place.along(self.turn(part))
            ref = self.ref(part, u[2], u[1] + r, 0, 4)
            result += [
                self.copy(part, 2, ref, s, 6 + 2 * r + way) for way, s in enumerate((1, SIDE - 1))
            ]
        return result

    def far_plane(self, r):
        way = lax.div(r, 2)
        step = 1 + 2 * way
        result = []
        for part in range(3):
            u = self.place.along(self.turn(part))
            ref = self.ref(part, u[2] + SIDE - step, u[1] + r, 0, 4)
            result.append(self.copy(part, 2, ref, step, 14 + r))
        return result

    def side(self, ref, part, sem):
        return pltpu.make_async_remote_copy(
            src_ref=ref,
            dst_ref=ref,
            send_sem=self.sib_send.at[part, sem],
            recv_sem=self.sib_recv.at[part, sem],
            device_id=self.place.sibling(),
            device_id_type=MESH,
        )

    def side_own(self):
        result = []
        for part in range(3):
            u = self.place.along(self.turn(part))
            result.append(self.side(self.ref(part, u[2], 0, 0, 16), part, 0))
        return result

    def side_near(self, r):
        result = []
        for part in range(3):
            u = self.place.along(self.turn(part))
            for way, plane in enumerate((3, 1)):
                ref = self.ref(part, u[2] + plane, u[1] + r, 0, 4)
                result.append(self.side(ref, part, 1 + 2 * r + way))
        return result

    def side_far(self, r):
        result = []
        for part in range(3):
            u = self.place.along(self.turn(part))
            result.append(self.side(self.ref(part, u[2] + 2, u[1] + r, 0, 4), part, 9 + r))
        return result

    def start(self, copies):
        for copy in copies:
            copy.start()

    def wait(self, copies):
        for copy in copies:
            copy.wait_recv()

    def second(self):
        self.wait(self.first(0))
        self.start(self.first(1))
        self.start(self.near_plane(0))

    def third(self):
        self.wait(self.first(1))
        for r in range(1, 4):
            self.start(self.near_plane(r))
        self.start(self.side_own())

    def pass_near(self, r):
        self.wait(self.near_plane(r))
        self.start(self.far_plane(r))
        self.start(self.side_near(r))

    def pass_far(self, r):
        self.wait(self.far_plane(r))
        self.start(self.side_far(r))

    def own_rows(self):
        rows = []
        for part in range(3):
            u = self.place.along(self.turn(part))
            start = self.start_row(part, u[2] * 16 + u[1] * 4 + u[0])
            for unit in range(PART_UNITS[part]):
                rows.append(lax.div(start + unit * RANK, LINES))
        return rows

    def finish_sends(self):
        for copy in self.first(0) + self.first(1) + self.side_own():
            copy.wait_send()

        def step(r, carry):
            copies = self.near_plane(r) + self.far_plane(r) + self.side_near(r) + self.side_far(r)
            for copy in copies:
                copy.wait_send()
            return carry

        lax.fori_loop(0, 4, step, 0)


def inverse_root(gram0, gram1):
    scales = [jnp.sqrt(jnp.sum(g * g) + EPSILON) for g in (gram0, gram1)]
    zero = jnp.zeros((RANK, RANK), f32)
    iterate = jnp.concatenate(
        [
            jnp.concatenate([gram0 / scales[0], zero], axis=1),
            jnp.concatenate([zero, gram1 / scales[1]], axis=1),
        ],
        axis=0,
    )
    shape = (2 * RANK, 2 * RANK)
    ident = jnp.where(
        lax.broadcasted_iota(jnp.int32, shape, 0) == lax.broadcasted_iota(jnp.int32, shape, 1),
        1.0,
        0.0,
    )
    root = ident
    for sweep in range(NSWEEPS):
        product = iterate if sweep == 0 else dot(root, iterate, ((1,), (0,)), HIGHEST)
        factor = 1.5 * ident - 0.5 * product
        if sweep < NSWEEPS - 1:
            iterate = dot(iterate, factor, ((1,), (0,)), HIGHEST)
        root = factor if sweep == 0 else dot(factor, root, ((1,), (0,)), HIGHEST)
    return root, scales


def kernel(
    coords, panel, mixing, owners, picks, bases_out, coup_out,
    in_ref, x_ref, pre_ref, q_ref, b_ref, k_ref, g_ref, gt_ref, l_ref, bs_ref, sc_ref, sct_ref, st_ref,
    in_sem, q_send, q_recv, q_sib_send, q_sib_recv, b_send, b_recv, b_sib_send, b_sib_recv,
):
    place = Place()
    gather_q = Gather(place, q_ref, q_send, q_recv, q_sib_send, q_sib_recv)
    gather_b = Gather(place, b_ref, b_send, b_recv, b_sib_send, b_sib_recv)

    width = coords.shape[1] // INPUTS

    def load(j):
        return pltpu.make_async_copy(
            coords.at[:, j * width : (j + 1) * width], in_ref.at[j % 2], in_sem.at[j % 2]
        )

    load(0).start()
    load(1).start()
    barrier = pltpu.get_barrier_semaphore()
    peers = [place.neighbour(axis, step) for axis in range(3) for step in (1, 2, 3)]
    peers.append(place.sibling())
    for peer in peers:
        pl.semaphore_signal(barrier, inc=1, device_id=peer, device_id_type=MESH)

    vectors = dot(mixing[...], panel[...].astype(f32), ((1,), (1,)), HIGHEST).astype(bf16)
    for unit, row in enumerate(gather_q.own_rows()):
        for n in range(2):
            q_ref[row + n] = vectors[LINES * n : LINES * (n + 1), unit * UNIT : (unit + 1) * UNIT]
    pl.semaphore_wait(barrier, len(peers))

    gather_q.start(gather_q.first(0))
    for j in range(INPUTS):
        load(j).wait()
        for unit in range(width // UNIT):
            x_ref[j * width // UNIT + unit] = in_ref[j % 2, :, unit * UNIT : (unit + 1) * UNIT]
        if j + 2 < INPUTS:
            load(j + 2).start()
    own = [x_ref[place.index * UNITS + unit] for unit in range(UNITS)]
    own_features = features(jnp.concatenate(own, axis=1), False)
    g_ref[...] = own_features
    for leaf in range(2):
        gt_ref[leaf] = own_features[:, leaf * LEAF : (leaf + 1) * LEAF].T

    def pair_step(g, carry):
        @pl.when(g == 6)
        def _():
            gather_q.second()

        far = []
        for n in range(GROUP):
            entry = (owners[0, g * GROUP + n] * 2 + picks[1, g * GROUP + n]) * 2
            far += [x_ref[entry], x_ref[entry + 1]]
        far = features(jnp.concatenate(far, axis=1), True)
        for n in range(GROUP):
            near_rows = gt_ref[picks[0, g * GROUP + n]]
            exponent = dot(near_rows, far[:, n * LEAF : (n + 1) * LEAF], ((1,), (0,)))
            k_ref[g * GROUP + n] = jnp.exp2(exponent).astype(bf16)
        return carry

    lax.fori_loop(0, PAIRS // GROUP, pair_step, 0)

    def chunk(i):
        in_own, in_far = i < 4, i >= 12
        other = jnp.where(in_own, lax.div(i, 2), lax.rem(i, 2))
        core = lax.rem(place.core + other, 2)
        r = jnp.where(in_far, lax.div(i + 4, 2) - 8, jnp.where(in_own, 2 * lax.rem(i, 2), lax.div(i, 2) - 2))
        groups = (r, r + jnp.where(in_far, 2, jnp.where(in_own, 1, 0)))
        planes = [jnp.where(in_far, 2, jnp.where(in_own, 0, p)) for p in (3, 1)]
        units = []
        for half in range(2):
            for unit in range(UNITS):
                part = max(unit - 1, 0)
                turn = lax.rem(part + core, 3)
                w = [pick3(turn, *((4, 1, 32) * 2)[s : s + 3]) for s in range(3)]
                u = place.along(turn)
                u2, u1 = lax.rem(u[2] + planes[half], SIDE), lax.rem(u[1] + groups[half], SIDE)
                device = core * 16 + u2 * w[2] + u1 * w[1]
                entry = core * (CORE_ROWS // LINES) + PART_BASE[part] // LINES
                size = PART_ROWS[part] // LINES
                entry = entry + (u2 * 16 + u1 * 4) * size + (unit % 2 if part == 0 else 0) * 2
                for u0 in range(SIDE):
                    units.append(((device + u0 * w[0]) * UNITS + unit, entry + u0 * size))
        return units

    def chunk_tile(i):
        columns = features(jnp.concatenate([x_ref[p] for p, _ in chunk(i)], axis=1), True).T
        return jnp.exp2(dot(columns, g_ref[...], ((1,), (0,)))).astype(bf16)

    def chunk_vectors(i):
        vectors = [jnp.concatenate([q_ref[v], q_ref[v + 1]], axis=0) for _, v in chunk(i)]
        return jnp.concatenate(vectors, axis=1)

    def early_tile(i, carry):
        pre_ref[i] = chunk_tile(i)
        return carry

    lax.fori_loop(0, EARLY, early_tile, 0)
    gather_q.third()

    def await_side(i):
        @pl.when(i == 2)
        def _():
            gather_q.wait(gather_q.side_own())

    def early_step(i, total):
        await_side(i)
        return total + dot(chunk_vectors(i), pre_ref[i], ((1,), (0,)))

    total = lax.fori_loop(0, EARLY, early_step, jnp.zeros((RANK, OWN), f32))

    def sketch_step(i, total):
        await_side(i)
        even = lax.rem(i, 2) == 0

        @pl.when((i >= 4) & (i < 12) & even)
        def _():
            gather_q.pass_near(lax.div(i, 2) - 2)

        @pl.when((i >= 4) & (i < 12) & jnp.logical_not(even))
        def _():
            gather_q.wait(gather_q.side_near(lax.div(i, 2) - 2))

        @pl.when((i >= 12) & even)
        def _():
            gather_q.pass_far(lax.div(i, 2) - 6)
            gather_q.pass_far(lax.div(i, 2) - 4)

        @pl.when((i >= 12) & jnp.logical_not(even))
        def _():
            gather_q.wait(gather_q.side_far(lax.div(i, 2) - 6))
            gather_q.wait(gather_q.side_far(lax.div(i, 2) - 4))

        tile = chunk_tile(i)
        return total + dot(chunk_vectors(i), tile, ((1,), (0,)))

    narrow = lax.fori_loop(EARLY, 16, sketch_step, total)

    grams = [dot(n, n, ((1,), (1,)), HIGHEST) for n in (narrow[:, :LEAF], narrow[:, LEAF:])]
    root, scales = inverse_root(*grams)
    stacked = jnp.concatenate([narrow[:, :LEAF], narrow[:, LEAF:]], axis=0)
    left = lax.broadcasted_iota(jnp.int32, (1, 2 * RANK), 1) < RANK
    scale = jnp.sqrt(jnp.where(left, scales[0], scales[1]))
    rounded = (dot(stacked, root, ((0,), (0,)), HIGHEST) / scale).astype(bf16)
    for unit, row in enumerate(gather_b.own_rows()):
        for n in range(2):
            at = unit * RANK + LINES * n
            b_ref[row + n] = rounded[at : at + LINES, :]
    gather_b.start(gather_b.first(0))

    packed = rounded.astype(f32)
    sc_ref[...] = packed
    flipped = packed.T
    for side in range(2):
        sct_ref[128 * side : 128 * (side + 1), :] = flipped[:, 128 * side : 128 * (side + 1)]
    even, odd = sc_ref[pl.ds(0, 128, stride=2), :], sc_ref[pl.ds(1, 128, stride=2), :]
    bases_out[0] = jnp.where(left, even, pltpu.roll(odd, RANK, 1)).astype(bf16)
    bases_out[1] = jnp.where(left, pltpu.roll(even, RANK, 1), odd).astype(bf16)
    half = RANK // 2
    for leaf in range(2):
        for odd_one in range(2):
            at = odd_one * half
            for side in range(2):
                first = 128 * side + leaf * RANK + odd_one
                bs_ref[leaf, at : at + half, 128 * side : 128 * (side + 1)] = sct_ref[
                    pl.ds(first, half, stride=2), :
                ].astype(bf16)

    def near_step(g, carry):
        for n in range(GROUP):
            k = g * GROUP + n
            l_ref[k] = dot(bs_ref[picks[0, k]], k_ref[k], ((1,), (0,))).astype(bf16)
        return carry

    lax.fori_loop(0, PAIRS // GROUP, near_step, 0)

    gather_b.second()
    gather_b.third()

    def near_planes(r, carry):
        gather_b.pass_near(r)
        return carry

    def far_planes(r, carry):
        gather_b.pass_far(r)
        return carry

    def siblings(r, carry):
        gather_b.wait(gather_b.side_near(r))
        gather_b.wait(gather_b.side_far(r))
        return carry

    lax.fori_loop(0, 4, near_planes, 0)
    lax.fori_loop(0, 4, far_planes, 0)
    gather_b.wait(gather_b.side_own())
    lax.fori_loop(0, 4, siblings, 0)

    def far_step(g, carry):
        for pair in range(GROUP):
            k = g * GROUP + pair
            line, col = lax.div(owners[0, k], 16), lax.rem(owners[0, k], 16)
            core, z = lax.rem(line, 2), lax.div(line, 2)
            x, y = lax.div(col, SIDE), lax.rem(col, SIDE)
            slots = [z * 16 + y * 4 + x, x * 16 + z * 4 + y, y * 16 + x * 4 + z]
            blocks = []
            for part in range(3):
                slot = slots[part] + core * (slots[(part + 1) % 3] - slots[part])
                row = core * (CORE_ROWS // LINES) + PART_BASE[part] // LINES + slot * (PART_ROWS[part] // LINES)
                for n in range(PART_ROWS[part] // LINES):
                    blocks.append(b_ref[row + n])
            both = dot(
                l_ref[k],
                jnp.concatenate(blocks, axis=0),
                ((1,), (0,)),
            )
            even, odd = both[:half, :], both[half:, :]
            first = jnp.where(left, even, pltpu.roll(odd, RANK, 1))
            second = jnp.where(left, pltpu.roll(even, RANK, 1), odd)
            pick = picks[1, k].astype(f32)
            st_ref[pair * half : (pair + 1) * half, :] = first * (1.0 - pick) + second * pick
        rows = pl.ds(pl.multiple_of(g * GROUP, GROUP), GROUP)
        for i in range(half):
            coup_out[rows, 128 * i : 128 * (i + 1)] = st_ref[pl.ds(i, GROUP, stride=half), :]
        return carry

    lax.fori_loop(0, PAIRS // GROUP, far_step, 0)
    gather_q.finish_sends()
    gather_b.finish_sends()


def per_device(coords, panel, mixing, owners, leaf_picks):
    vmem = pl.BlockSpec(memory_space=pltpu.VMEM)
    smem = pl.BlockSpec(memory_space=pltpu.SMEM)
    sems = pltpu.SemaphoreType.DMA
    points = coords.shape[1]
    bases, couplings = pl.pallas_call(
        kernel,
        out_shape=(
            jax.ShapeDtypeStruct((2, 128, 128), bf16),
            jax.ShapeDtypeStruct((PAIRS, RANK * RANK), f32),
        ),
        in_specs=[pl.BlockSpec(memory_space=pl.ANY), vmem, vmem, smem, smem],
        out_specs=(vmem, vmem),
        scratch_shapes=[
            pltpu.VMEM((2, coords.shape[0], points // INPUTS), f32),
            pltpu.VMEM((points // UNIT, coords.shape[0], UNIT), f32),
            pltpu.VMEM((EARLY, CHUNK, OWN), bf16),
            pltpu.VMEM((2 * CORE_ROWS // LINES, LINES, 128), bf16),
            pltpu.VMEM((2 * CORE_ROWS // LINES, LINES, 128), bf16),
            pltpu.VMEM((PAIRS, LEAF, LEAF), bf16),
            pltpu.VMEM((128, OWN), bf16),
            pltpu.VMEM((2, LEAF, 128), bf16),
            pltpu.VMEM((PAIRS, RANK, LEAF), bf16),
            pltpu.VMEM((2, RANK, LEAF), bf16),
            pltpu.VMEM((LEAF, 128), f32),
            pltpu.VMEM((2 * 128, 128), f32),
            pltpu.VMEM((GROUP * RANK // 2, 128), f32),
            sems((2,)),
            sems((3, 18)),
            sems((3, 18)),
            sems((3, 13)),
            sems((3, 13)),
            sems((3, 18)),
            sems((3, 18)),
            sems((3, 13)),
            sems((3, 13)),
        ],
        compiler_params=pltpu.CompilerParams(
            collective_id=0, has_side_effects=True, vmem_limit_bytes=60 * 2**20
        ),
    )(coords, panel, mixing.T, owners.T, leaf_picks.T)
    return bases.reshape(2, LEAF * RANK), couplings


def solution(mesh):
    return jax.shard_map(
        per_device,
        mesh=mesh,
        in_specs=(
            P(),
            P(("row", "col"), None),
            P(),
            P(("row", "col"), None),
            P(("row", "col"), None),
        ),
        out_specs=(P(("row", "col"), None), P(("row", "col"), None)),
        check_vma=False,
    )
```

```python
import functools
import math

import jax
import jax.numpy as jnp
from jax import lax
from jax.experimental import pallas as pl
from jax.experimental.pallas import tpu as pltpu
from jax.sharding import PartitionSpec as P

MESH = pl.DeviceIdType.MESH
HIGHEST = lax.Precision.HIGHEST
f32, bf16 = jnp.float32, jnp.bfloat16

LEAF = 256
RANK = 64
NSWEEPS = 6
EPSILON = 1e-06
OWN = 512
UNIT = 128
UNITS = 4
PAIRS = 64
GROUP = 8
LINES = 32
SIDE = 4
CHUNK = 4096
EARLY = 3
INPUTS = 8
PART_UNITS = (2, 1, 1)
PART_ROWS = tuple(RANK * u for u in PART_UNITS)
PART_BASE = (0, 128 * SIDE**3, 192 * SIDE**3)
CORE_ROWS = 256 * SIDE**3


def dot(a, b, dims, precision=None):
    return lax.dot_general(
        a, b, (dims, ((), ())), precision=precision, preferred_element_type=f32
    )


def pick3(k, a, b, c):
    return jnp.where(k == 0, a, jnp.where(k == 1, b, c))


def back(j):
    return jnp.where(j == 0, 0, lax.rem(j, 3) + 1)


def split3(v):
    hi = v.astype(bf16)
    rest = v - hi.astype(f32)
    mid = rest.astype(bf16)
    lo = (rest - mid.astype(f32)).astype(bf16)
    return hi, mid, lo


def features(x, column):
    n = x.shape[1]
    a = x * math.sqrt(4.0 * math.log2(math.e) / x.shape[0])
    h = -0.5 * jnp.sum(a * a, axis=0, keepdims=True)
    hi, mid, lo = split3(a)
    parts = [jnp.broadcast_to(v.astype(f32), (16, n)) for v in split3(h)]
    line = lax.broadcasted_iota(jnp.int32, (16, n), 0)
    at = 0 if column else 3
    extra = jnp.where(line < 6, 1.0, 0.0)
    for k in range(3):
        extra = jnp.where(line == at + k, parts[k], extra)
    extra = extra.astype(bf16)
    zero = jnp.zeros((16, n), bf16)
    if column:
        stack = [hi, hi, mid, mid, hi, lo, extra, zero]
    else:
        stack = [hi, mid, hi, mid, lo, hi, extra, zero]
    return jnp.concatenate(stack, axis=0)


class Place:
    def __init__(self):
        row, col = lax.axis_index("row"), lax.axis_index("col")
        self.core = lax.rem(row, 2)
        self.z = lax.div(row, 2)
        self.x = lax.div(col, SIDE)
        self.y = lax.rem(col, SIDE)
        self.index = row * SIDE * SIDE + col

    def sibling(self):
        return (self.z * 2 + 1 - self.core, self.x * SIDE + self.y)

    def neighbour(self, axis, step):
        x = lax.rem(self.x + jnp.where(axis == 0, step, 0), SIDE)
        y = lax.rem(self.y + jnp.where(axis == 1, step, 0), SIDE)
        z = lax.rem(self.z + jnp.where(axis == 2, step, 0), SIDE)
        return (z * 2 + self.core, x * SIDE + y)

    def along(self, turn):
        c = (self.x, self.y, self.z)
        return [pick3(turn, c[s], c[(s + 1) % 3], c[(s + 2) % 3]) for s in range(3)]


class Gather:
    def __init__(self, place, buf, send, recv, sib_send, sib_recv):
        self.place, self.buf = place, buf
        self.send, self.recv = send, recv
        self.sib_send, self.sib_recv = sib_send, sib_recv

    def turn(self, part):
        return lax.rem(part + self.place.core, 3)

    def start_row(self, part, slot):
        return self.place.core * CORE_ROWS + PART_BASE[part] + slot * PART_ROWS[part]

    def ref(self, part, plane, group, slot, slots):
        first = lax.rem(plane, SIDE) * 16 + lax.rem(group, SIDE) * 4 + slot
        start = lax.div(self.start_row(part, first), LINES)
        return self.buf.at[pl.ds(start, slots * PART_ROWS[part] // LINES)]

    def copy(self, part, stage, ref, step, sem):
        return pltpu.make_async_remote_copy(
            src_ref=ref,
            dst_ref=ref,
            send_sem=self.send.at[part, sem],
            recv_sem=self.recv.at[part, sem],
            device_id=self.place.neighbour(lax.rem(self.turn(part) + stage, 3), step),
            device_id_type=MESH,
        )

    def first(self, stage):
        result = []
        for part in range(3):
            u = self.place.along(self.turn(part))
            ref = self.ref(part, u[2], u[1], u[0] if stage == 0 else 0, 1 if stage == 0 else 4)
            result += [self.copy(part, stage, ref, s, 3 * stage + s - 1) for s in (1, 2, 3)]
        return result

    def near_plane(self, j):
        result = []
        for part in range(3):
            u = self.place.along(self.turn(part))
            for way, (r, s) in enumerate(((j, 1), (back(j), SIDE - 1))):
                ref = self.ref(part, u[2], u[1] + r, 0, 4)
                result.append(self.copy(part, 2, ref, s, 6 + 2 * j + way))
        return result

    def far_plane(self, r):
        step = 1 + 2 * lax.div(r, 2)
        result = []
        for part in range(3):
            u = self.place.along(self.turn(part))
            ref = self.ref(part, u[2] + SIDE - step, u[1] + r, 0, 4)
            result.append(self.copy(part, 2, ref, step, 14 + r))
        return result

    def side(self, ref, part, sem):
        return pltpu.make_async_remote_copy(
            src_ref=ref,
            dst_ref=ref,
            send_sem=self.sib_send.at[part, sem],
            recv_sem=self.sib_recv.at[part, sem],
            device_id=self.place.sibling(),
            device_id_type=MESH,
        )

    def side_own(self):
        result = []
        for part in range(3):
            u = self.place.along(self.turn(part))
            result.append(self.side(self.ref(part, u[2], 0, 0, 16), part, 0))
        return result

    def side_near(self, j):
        result = []
        for part in range(3):
            u = self.place.along(self.turn(part))
            for way, (r, plane) in enumerate(((j, 3), (back(j), 1))):
                ref = self.ref(part, u[2] + plane, u[1] + r, 0, 4)
                result.append(self.side(ref, part, 1 + 2 * j + way))
        return result

    def side_far(self, r):
        result = []
        for part in range(3):
            u = self.place.along(self.turn(part))
            result.append(self.side(self.ref(part, u[2] + 2, u[1] + r, 0, 4), part, 9 + r))
        return result

    def start(self, copies):
        for copy in copies:
            copy.start()

    def wait(self, copies):
        for copy in copies:
            copy.wait_recv()

    def second(self):
        self.wait(self.first(0))
        self.start(self.first(1))
        self.start(self.near_plane(0))

    def third(self):
        self.wait(self.first(1))
        for r in range(1, 4):
            self.start(self.near_plane(r))
        self.start(self.side_own())

    def pass_near(self, j):
        self.wait(self.near_plane(j))
        for r, when in enumerate((0, 1, 1, 2)):

            @pl.when(j == when)
            def _(r=r):
                self.start(self.far_plane(r))

        self.start(self.side_near(j))

    def pass_far(self, r):
        self.wait(self.far_plane(r))
        self.start(self.side_far(r))

    def own_rows(self):
        rows = []
        for part in range(3):
            u = self.place.along(self.turn(part))
            start = self.start_row(part, u[2] * 16 + u[1] * 4 + u[0])
            for unit in range(PART_UNITS[part]):
                rows.append(lax.div(start + unit * RANK, LINES))
        return rows

    def finish_sends(self):
        for copy in self.first(0) + self.first(1) + self.side_own():
            copy.wait_send()

        def step(r, carry):
            copies = self.near_plane(r) + self.far_plane(r) + self.side_near(r) + self.side_far(r)
            for copy in copies:
                copy.wait_send()
            return carry

        lax.fori_loop(0, 4, step, 0)


def dot3(a, b):
    ah, bh = a.astype(bf16), b.astype(bf16)
    al, bl = (a - ah.astype(f32)).astype(bf16), (b - bh.astype(f32)).astype(bf16)
    by = ((1,), (0,))
    return dot(ah, bh, by) + (dot(ah, bl, by) + dot(al, bh, by))


def inverse_root(stacked, left):
    shape = (2 * RANK, 2 * RANK)
    row = lax.broadcasted_iota(jnp.int32, shape, 0)
    col = lax.broadcasted_iota(jnp.int32, shape, 1)
    gram = jnp.where((row < RANK) == (col < RANK), dot(stacked, stacked, ((1,), (1,)), HIGHEST), 0.0)
    sums = jnp.sum(gram * gram, axis=0, keepdims=True)
    zero = jnp.zeros_like(sums)
    sums = [jnp.sum(v, axis=1, keepdims=True) for v in (jnp.where(left, sums, zero), jnp.where(left, zero, sums))]
    scale = jnp.sqrt(jnp.where(left, sums[0], sums[1]) + EPSILON)
    iterate = gram / scale
    ident = jnp.where(row == col, 1.0, 0.0)
    root = ident
    for sweep in range(NSWEEPS):
        product = iterate if sweep == 0 else dot3(root, iterate)
        factor = 1.5 * ident - 0.5 * product
        if sweep < NSWEEPS - 1:
            iterate = dot3(iterate, factor)
        root = factor if sweep == 0 else dot3(factor, root)
    return root, scale


def kernel(
    coords, panel, mixing, owners, picks, bases_out, coup_out,
    in_ref, x_ref, pre_ref, q_ref, b_ref, k_ref, g_ref, gt_ref, l_ref, bs_ref, sc_ref, sct_ref, st_ref,
    in_sem, q_send, q_recv, q_sib_send, q_sib_recv, b_send, b_recv, b_sib_send, b_sib_recv,
):
    place = Place()
    gather_q = Gather(place, q_ref, q_send, q_recv, q_sib_send, q_sib_recv)
    gather_b = Gather(place, b_ref, b_send, b_recv, b_sib_send, b_sib_recv)

    width = coords.shape[1] // INPUTS

    def load(j):
        return pltpu.make_async_copy(
            coords.at[:, j * width : (j + 1) * width], in_ref.at[j % 4], in_sem.at[j % 4]
        )

    for j in range(4):
        load(j).start()
    barrier = pltpu.get_barrier_semaphore()
    peers = [place.neighbour(axis, step) for axis in range(3) for step in (1, 2, 3)]
    peers.append(place.sibling())
    for peer in peers:
        pl.semaphore_signal(barrier, inc=1, device_id=peer, device_id_type=MESH)

    vectors = dot(mixing[...], panel[...].astype(f32), ((1,), (1,)), HIGHEST).astype(bf16)
    for unit, row in enumerate(gather_q.own_rows()):
        for n in range(2):
            q_ref[row + n] = vectors[LINES * n : LINES * (n + 1), unit * UNIT : (unit + 1) * UNIT]
    pl.semaphore_wait(barrier, len(peers))

    gather_q.start(gather_q.first(0))
    for j in range(INPUTS):
        load(j).wait()
        for unit in range(width // UNIT):
            x_ref[j * width // UNIT + unit] = in_ref[j % 4, :, unit * UNIT : (unit + 1) * UNIT]
        if j + 4 < INPUTS:
            load(j + 4).start()
    own = [x_ref[place.index * UNITS + unit] for unit in range(UNITS)]
    own_features = features(jnp.concatenate(own, axis=1), False)
    g_ref[...] = own_features
    for leaf in range(2):
        gt_ref[leaf] = own_features[:, leaf * LEAF : (leaf + 1) * LEAF].T

    def pair_step(g, carry):
        @pl.when(g == 6)
        def _():
            gather_q.second()

        far = []
        for n in range(GROUP):
            entry = (owners[0, g * GROUP + n] * 2 + picks[1, g * GROUP + n]) * 2
            far += [x_ref[entry], x_ref[entry + 1]]
        far = features(jnp.concatenate(far, axis=1), True)
        for n in range(GROUP):
            near_rows = gt_ref[picks[0, g * GROUP + n]]
            exponent = dot(near_rows, far[:, n * LEAF : (n + 1) * LEAF], ((1,), (0,)))
            k_ref[g * GROUP + n] = jnp.exp2(exponent).astype(bf16)
        return carry

    lax.fori_loop(0, PAIRS // GROUP, pair_step, 0)

    def chunk(i):
        in_own, in_far = i < 4, i >= 12
        other = jnp.where(in_own, lax.div(i, 2), lax.rem(i, 2))
        core = lax.rem(place.core + other, 2)
        r = jnp.where(in_far, lax.div(i + 4, 2) - 8, jnp.where(in_own, 2 * lax.rem(i, 2), lax.div(i, 2) - 2))
        groups = (r, jnp.where(in_far, r + 2, jnp.where(in_own, r + 1, back(r))))
        planes = [jnp.where(in_far, 2, jnp.where(in_own, 0, p)) for p in (3, 1)]
        units = []
        for half in range(2):
            for unit in range(UNITS):
                part = max(unit - 1, 0)
                turn = lax.rem(part + core, 3)
                w = [pick3(turn, *((4, 1, 32) * 2)[s : s + 3]) for s in range(3)]
                u = place.along(turn)
                u2, u1 = lax.rem(u[2] + planes[half], SIDE), lax.rem(u[1] + groups[half], SIDE)
                device = core * 16 + u2 * w[2] + u1 * w[1]
                entry = core * (CORE_ROWS // LINES) + PART_BASE[part] // LINES
                size = PART_ROWS[part] // LINES
                entry = entry + (u2 * 16 + u1 * 4) * size + (unit % 2 if part == 0 else 0) * 2
                for u0 in range(SIDE):
                    units.append(((device + u0 * w[0]) * UNITS + unit, entry + u0 * size))
        return units

    def chunk_tile(i):
        columns = features(jnp.concatenate([x_ref[p] for p, _ in chunk(i)], axis=1), True).T
        return jnp.exp2(dot(columns, g_ref[...], ((1,), (0,)))).astype(bf16)

    def chunk_vectors(i):
        vectors = [jnp.concatenate([q_ref[v], q_ref[v + 1]], axis=0) for _, v in chunk(i)]
        return jnp.concatenate(vectors, axis=1)

    def early_tile(i, carry):
        pre_ref[i] = chunk_tile(i)
        return carry

    lax.fori_loop(0, EARLY, early_tile, 0)
    gather_q.third()

    def await_side(i):
        @pl.when(i == 2)
        def _():
            gather_q.wait(gather_q.side_own())

    def early_step(i, total):
        await_side(i)
        return total + dot(chunk_vectors(i), pre_ref[i], ((1,), (0,)))

    total = lax.fori_loop(0, EARLY, early_step, jnp.zeros((RANK, OWN), f32))

    def sketch_step(i, total):
        await_side(i)
        even = lax.rem(i, 2) == 0

        @pl.when((i >= 4) & (i < 12) & even)
        def _():
            gather_q.pass_near(lax.div(i, 2) - 2)

        @pl.when((i >= 4) & (i < 12) & jnp.logical_not(even))
        def _():
            gather_q.wait(gather_q.side_near(lax.div(i, 2) - 2))

        @pl.when((i >= 12) & even)
        def _():
            gather_q.pass_far(lax.div(i, 2) - 6)
            gather_q.pass_far(lax.div(i, 2) - 4)

        @pl.when((i >= 12) & jnp.logical_not(even))
        def _():
            gather_q.wait(gather_q.side_far(lax.div(i, 2) - 6))
            gather_q.wait(gather_q.side_far(lax.div(i, 2) - 4))

        tile = chunk_tile(i)
        return total + dot(chunk_vectors(i), tile, ((1,), (0,)))

    narrow = lax.fori_loop(EARLY, 16, sketch_step, total)

    stacked = jnp.concatenate([narrow[:, :LEAF], narrow[:, LEAF:]], axis=0)
    left = lax.broadcasted_iota(jnp.int32, (1, 2 * RANK), 1) < RANK
    root, scale = inverse_root(stacked, left)
    scale = jnp.sqrt(scale)
    rounded = (dot(stacked, root, ((0,), (0,)), HIGHEST) / scale).astype(bf16)
    for unit, row in enumerate(gather_b.own_rows()):
        for n in range(2):
            at = unit * RANK + LINES * n
            b_ref[row + n] = rounded[at : at + LINES, :]
    gather_b.start(gather_b.first(0))

    packed = rounded.astype(f32)
    sc_ref[...] = packed
    flipped = packed.T
    for side in range(2):
        sct_ref[128 * side : 128 * (side + 1), :] = flipped[:, 128 * side : 128 * (side + 1)]
    even, odd = sc_ref[pl.ds(0, 128, stride=2), :], sc_ref[pl.ds(1, 128, stride=2), :]
    bases_out[0] = jnp.where(left, even, pltpu.roll(odd, RANK, 1)).astype(bf16)
    bases_out[1] = jnp.where(left, pltpu.roll(even, RANK, 1), odd).astype(bf16)
    half = RANK // 2
    for leaf in range(2):
        for odd_one in range(2):
            at = odd_one * half
            for side in range(2):
                first = 128 * side + leaf * RANK + odd_one
                bs_ref[leaf, at : at + half, 128 * side : 128 * (side + 1)] = sct_ref[
                    pl.ds(first, half, stride=2), :
                ].astype(bf16)

    def near_step(g, carry):
        for n in range(GROUP):
            k = g * GROUP + n
            l_ref[k] = dot(bs_ref[picks[0, k]], k_ref[k], ((1,), (0,))).astype(bf16)
        return carry

    lax.fori_loop(0, PAIRS // GROUP, near_step, 0)

    gather_b.second()
    gather_b.third()

    def near_planes(r, carry):
        gather_b.pass_near(r)
        return carry

    def far_planes(r, carry):
        gather_b.pass_far(r)
        return carry

    def siblings(r, carry):
        gather_b.wait(gather_b.side_near(r))
        gather_b.wait(gather_b.side_far(r))
        return carry

    lax.fori_loop(0, 4, near_planes, 0)
    lax.fori_loop(0, 4, far_planes, 0)
    gather_b.wait(gather_b.side_own())
    lax.fori_loop(0, 4, siblings, 0)

    def far_step(g, carry):
        for pair in range(GROUP):
            k = g * GROUP + pair
            line, col = lax.div(owners[0, k], 16), lax.rem(owners[0, k], 16)
            core, z = lax.rem(line, 2), lax.div(line, 2)
            x, y = lax.div(col, SIDE), lax.rem(col, SIDE)
            slots = [z * 16 + y * 4 + x, x * 16 + z * 4 + y, y * 16 + x * 4 + z]
            blocks = []
            for part in range(3):
                slot = slots[part] + core * (slots[(part + 1) % 3] - slots[part])
                row = core * (CORE_ROWS // LINES) + PART_BASE[part] // LINES + slot * (PART_ROWS[part] // LINES)
                for n in range(PART_ROWS[part] // LINES):
                    blocks.append(b_ref[row + n])
            both = dot(
                l_ref[k],
                jnp.concatenate(blocks, axis=0),
                ((1,), (0,)),
            )
            even, odd = both[:half, :], both[half:, :]
            first = jnp.where(left, even, pltpu.roll(odd, RANK, 1))
            second = jnp.where(left, pltpu.roll(even, RANK, 1), odd)
            pick = picks[1, k].astype(f32)
            st_ref[pair * half : (pair + 1) * half, :] = first * (1.0 - pick) + second * pick
        rows = pl.ds(pl.multiple_of(g * GROUP, GROUP), GROUP)
        for i in range(half):
            coup_out[rows, 128 * i : 128 * (i + 1)] = st_ref[pl.ds(i, GROUP, stride=half), :]
        return carry

    lax.fori_loop(0, PAIRS // GROUP, far_step, 0)
    gather_q.finish_sends()
    gather_b.finish_sends()


def per_device(coords, panel, mixing, owners, leaf_picks):
    vmem = pl.BlockSpec(memory_space=pltpu.VMEM)
    smem = pl.BlockSpec(memory_space=pltpu.SMEM)
    sems = pltpu.SemaphoreType.DMA
    points = coords.shape[1]
    bases, couplings = pl.pallas_call(
        kernel,
        out_shape=(
            jax.ShapeDtypeStruct((2, 128, 128), bf16),
            jax.ShapeDtypeStruct((PAIRS, RANK * RANK), f32),
        ),
        in_specs=[pl.BlockSpec(memory_space=pl.ANY), vmem, vmem, smem, smem],
        out_specs=(vmem, vmem),
        scratch_shapes=[
            pltpu.VMEM((4, coords.shape[0], points // INPUTS), f32),
            pltpu.VMEM((points // UNIT, coords.shape[0], UNIT), f32),
            pltpu.VMEM((EARLY, CHUNK, OWN), bf16),
            pltpu.VMEM((2 * CORE_ROWS // LINES, LINES, 128), bf16),
            pltpu.VMEM((2 * CORE_ROWS // LINES, LINES, 128), bf16),
            pltpu.VMEM((PAIRS, LEAF, LEAF), bf16),
            pltpu.VMEM((128, OWN), bf16),
            pltpu.VMEM((2, LEAF, 128), bf16),
            pltpu.VMEM((PAIRS, RANK, LEAF), bf16),
            pltpu.VMEM((2, RANK, LEAF), bf16),
            pltpu.VMEM((LEAF, 128), f32),
            pltpu.VMEM((2 * 128, 128), f32),
            pltpu.VMEM((GROUP * RANK // 2, 128), f32),
            sems((4,)),
            sems((3, 18)),
            sems((3, 18)),
            sems((3, 13)),
            sems((3, 13)),
            sems((3, 18)),
            sems((3, 18)),
            sems((3, 13)),
            sems((3, 13)),
        ],
        compiler_params=pltpu.CompilerParams(
            collective_id=0, has_side_effects=True, vmem_limit_bytes=60 * 2**20
        ),
    )(coords, panel, mixing.T, owners.T, leaf_picks.T)
    return bases.reshape(2, LEAF * RANK), couplings


def solution(mesh):
    return jax.shard_map(
        per_device,
        mesh=mesh,
        in_specs=(
            P(),
            P(("row", "col"), None),
            P(),
            P(("row", "col"), None),
            P(("row", "col"), None),
        ),
        out_specs=(P(("row", "col"), None), P(("row", "col"), None)),
        check_vma=False,
    )
```

```python
import functools
import math

import jax
import jax.numpy as jnp
from jax import lax
from jax.experimental import pallas as pl
from jax.experimental.pallas import tpu as pltpu
from jax.sharding import PartitionSpec as P

MESH = pl.DeviceIdType.MESH
HIGHEST = lax.Precision.HIGHEST
f32, bf16 = jnp.float32, jnp.bfloat16

LEAF = 256
RANK = 64
NSWEEPS = 6
EPSILON = 1e-06
OWN = 512
UNIT = 128
UNITS = 4
PAIRS = 64
GROUP = 8
LINES = 32
SIDE = 4
CHUNK = 4096
EARLY = 6
INPUTS = 16
PART_UNITS = (2, 1, 1)
PART_ROWS = tuple(RANK * u for u in PART_UNITS)
PART_BASE = (0, 128 * SIDE**3, 192 * SIDE**3)
CORE_ROWS = 256 * SIDE**3


def dot(a, b, dims, precision=None):
    return lax.dot_general(
        a, b, (dims, ((), ())), precision=precision, preferred_element_type=f32
    )


def pick3(k, a, b, c):
    return jnp.where(k == 0, a, jnp.where(k == 1, b, c))


def back(j):
    return jnp.where(j == 0, 0, lax.rem(j, 3) + 1)


def split3(v):
    hi = v.astype(bf16)
    rest = v - hi.astype(f32)
    mid = rest.astype(bf16)
    lo = (rest - mid.astype(f32)).astype(bf16)
    return hi, mid, lo


def features(x, column):
    n = x.shape[1]
    a = x * math.sqrt(4.0 * math.log2(math.e) / x.shape[0])
    h = -0.5 * jnp.sum(a * a, axis=0, keepdims=True)
    hi, mid, lo = split3(a)
    parts = [jnp.broadcast_to(v.astype(f32), (16, n)) for v in split3(h)]
    line = lax.broadcasted_iota(jnp.int32, (16, n), 0)
    at = 0 if column else 3
    extra = jnp.where(line < 6, 1.0, 0.0)
    for k in range(3):
        extra = jnp.where(line == at + k, parts[k], extra)
    extra = extra.astype(bf16)
    zero = jnp.zeros((16, n), bf16)
    if column:
        stack = [hi, hi, mid, mid, hi, lo, extra, zero]
    else:
        stack = [hi, mid, hi, mid, lo, hi, extra, zero]
    return jnp.concatenate(stack, axis=0)


class Place:
    def __init__(self):
        row, col = lax.axis_index("row"), lax.axis_index("col")
        self.core = lax.rem(row, 2)
        self.z = lax.div(row, 2)
        self.x = lax.div(col, SIDE)
        self.y = lax.rem(col, SIDE)
        self.index = row * SIDE * SIDE + col

    def sibling(self):
        return (self.z * 2 + 1 - self.core, self.x * SIDE + self.y)

    def neighbour(self, axis, step):
        x = lax.rem(self.x + jnp.where(axis == 0, step, 0), SIDE)
        y = lax.rem(self.y + jnp.where(axis == 1, step, 0), SIDE)
        z = lax.rem(self.z + jnp.where(axis == 2, step, 0), SIDE)
        return (z * 2 + self.core, x * SIDE + y)

    def along(self, turn):
        c = (self.x, self.y, self.z)
        return [pick3(turn, c[s], c[(s + 1) % 3], c[(s + 2) % 3]) for s in range(3)]


class Gather:
    def __init__(self, place, buf, send, recv, sib_send, sib_recv):
        self.place, self.buf = place, buf
        self.send, self.recv = send, recv
        self.sib_send, self.sib_recv = sib_send, sib_recv

    def turn(self, part):
        return lax.rem(part + self.place.core, 3)

    def start_row(self, part, slot):
        return self.place.core * CORE_ROWS + PART_BASE[part] + slot * PART_ROWS[part]

    def ref(self, part, plane, group, slot, slots):
        first = lax.rem(plane, SIDE) * 16 + lax.rem(group, SIDE) * 4 + slot
        start = lax.div(self.start_row(part, first), LINES)
        return self.buf.at[pl.ds(start, slots * PART_ROWS[part] // LINES)]

    def copy(self, part, stage, ref, step, sem):
        return pltpu.make_async_remote_copy(
            src_ref=ref,
            dst_ref=ref,
            send_sem=self.send.at[part, sem],
            recv_sem=self.recv.at[part, sem],
            device_id=self.place.neighbour(lax.rem(self.turn(part) + stage, 3), step),
            device_id_type=MESH,
        )

    def first(self, stage):
        result = []
        for part in range(3):
            u = self.place.along(self.turn(part))
            ref = self.ref(part, u[2], u[1], u[0] if stage == 0 else 0, 1 if stage == 0 else 4)
            result += [self.copy(part, stage, ref, s, 3 * stage + s - 1) for s in (1, 2, 3)]
        return result

    def near_plane(self, j):
        result = []
        for part in range(3):
            u = self.place.along(self.turn(part))
            for way, (r, s) in enumerate(((j, 1), (back(j), SIDE - 1))):
                ref = self.ref(part, u[2], u[1] + r, 0, 4)
                result.append(self.copy(part, 2, ref, s, 6 + 2 * j + way))
        return result

    def far_plane(self, r):
        step = 1 + 2 * lax.div(r, 2)
        result = []
        for part in range(3):
            u = self.place.along(self.turn(part))
            ref = self.ref(part, u[2] + SIDE - step, u[1] + r, 0, 4)
            result.append(self.copy(part, 2, ref, step, 14 + r))
        return result

    def side(self, ref, part, sem):
        return pltpu.make_async_remote_copy(
            src_ref=ref,
            dst_ref=ref,
            send_sem=self.sib_send.at[part, sem],
            recv_sem=self.sib_recv.at[part, sem],
            device_id=self.place.sibling(),
            device_id_type=MESH,
        )

    def side_own(self):
        result = []
        for part in range(3):
            u = self.place.along(self.turn(part))
            result.append(self.side(self.ref(part, u[2], 0, 0, 16), part, 0))
        return result

    def side_near(self, j):
        result = []
        for part in range(3):
            u = self.place.along(self.turn(part))
            for way, (r, plane) in enumerate(((j, 3), (back(j), 1))):
                ref = self.ref(part, u[2] + plane, u[1] + r, 0, 4)
                result.append(self.side(ref, part, 1 + 2 * j + way))
        return result

    def side_far(self, r):
        result = []
        for part in range(3):
            u = self.place.along(self.turn(part))
            result.append(self.side(self.ref(part, u[2] + 2, u[1] + r, 0, 4), part, 9 + r))
        return result

    def start(self, copies):
        for copy in copies:
            copy.start()

    def wait(self, copies):
        for copy in copies:
            copy.wait_recv()

    def second(self):
        self.wait(self.first(0))
        self.start(self.first(1))
        self.start(self.near_plane(0))

    def third(self):
        self.wait(self.first(1))
        for r in range(1, 4):
            self.start(self.near_plane(r))
        self.start(self.side_own())

    def pass_near(self, j):
        self.wait(self.near_plane(j))
        for r, when in enumerate((0, 1, 1, 2)):

            @pl.when(j == when)
            def _(r=r):
                self.start(self.far_plane(r))

        self.start(self.side_near(j))

    def pass_far(self, r):
        self.wait(self.far_plane(r))
        self.start(self.side_far(r))

    def own_rows(self):
        rows = []
        for part in range(3):
            u = self.place.along(self.turn(part))
            start = self.start_row(part, u[2] * 16 + u[1] * 4 + u[0])
            for unit in range(PART_UNITS[part]):
                rows.append(lax.div(start + unit * RANK, LINES))
        return rows

    def finish_sends(self):
        for copy in self.first(0) + self.first(1) + self.side_own():
            copy.wait_send()

        def step(r, carry):
            copies = self.near_plane(r) + self.far_plane(r) + self.side_near(r) + self.side_far(r)
            for copy in copies:
                copy.wait_send()
            return carry

        lax.fori_loop(0, 4, step, 0)


def dot3(a, b):
    ah, bh = a.astype(bf16), b.astype(bf16)
    al, bl = (a - ah.astype(f32)).astype(bf16), (b - bh.astype(f32)).astype(bf16)
    by = ((1,), (0,))
    return dot(ah, bh, by) + (dot(ah, bl, by) + dot(al, bh, by))


def inverse_root(stacked, left):
    shape = (2 * RANK, 2 * RANK)
    row = lax.broadcasted_iota(jnp.int32, shape, 0)
    col = lax.broadcasted_iota(jnp.int32, shape, 1)
    gram = jnp.where((row < RANK) == (col < RANK), dot(stacked, stacked, ((1,), (1,)), HIGHEST), 0.0)
    sums = jnp.sum(gram * gram, axis=0, keepdims=True)
    zero = jnp.zeros_like(sums)
    sums = [jnp.sum(v, axis=1, keepdims=True) for v in (jnp.where(left, sums, zero), jnp.where(left, zero, sums))]
    scale = jnp.sqrt(jnp.where(left, sums[0], sums[1]) + EPSILON)
    iterate = gram / scale
    ident = jnp.where(row == col, 1.0, 0.0)
    root = ident
    for sweep in range(NSWEEPS):
        product = iterate if sweep == 0 else dot3(root, iterate)
        factor = 1.5 * ident - 0.5 * product
        if sweep < NSWEEPS - 1:
            iterate = dot3(iterate, factor)
        root = factor if sweep == 0 else dot3(factor, root)
    return root, scale


def kernel(
    coords, panel, mixing, owners, picks, bases_out, coup_out,
    in_ref, x_ref, pre_ref, q_ref, b_ref, g_ref, gt_ref, l_ref, bs_ref, sc_ref, sct_ref, st_ref,
    in_sem, q_send, q_recv, q_sib_send, q_sib_recv, b_send, b_recv, b_sib_send, b_sib_recv,
):
    place = Place()
    gather_q = Gather(place, q_ref, q_send, q_recv, q_sib_send, q_sib_recv)
    gather_b = Gather(place, b_ref, b_send, b_recv, b_sib_send, b_sib_recv)

    width = coords.shape[1] // INPUTS

    def load(j):
        return pltpu.make_async_copy(
            coords.at[:, j * width : (j + 1) * width], in_ref.at[j % 4], in_sem.at[j % 4]
        )

    for j in range(4):
        load(j).start()
    barrier = pltpu.get_barrier_semaphore()
    peers = [place.neighbour(axis, step) for axis in range(3) for step in (1, 2, 3)]
    peers.append(place.sibling())
    for peer in peers:
        pl.semaphore_signal(barrier, inc=1, device_id=peer, device_id_type=MESH)

    vectors = dot(mixing[...], panel[...].astype(f32), ((1,), (1,)), HIGHEST).astype(bf16)
    for unit, row in enumerate(gather_q.own_rows()):
        for n in range(2):
            q_ref[row + n] = vectors[LINES * n : LINES * (n + 1), unit * UNIT : (unit + 1) * UNIT]
    for j in range(INPUTS):
        load(j).wait()
        for unit in range(width // UNIT):
            x_ref[j * width // UNIT + unit] = in_ref[j % 4, :, unit * UNIT : (unit + 1) * UNIT]
        if j + 4 < INPUTS:
            load(j + 4).start()
    own = [x_ref[place.index * UNITS + unit] for unit in range(UNITS)]
    own_features = features(jnp.concatenate(own, axis=1), False)
    g_ref[...] = own_features
    for leaf in range(2):
        gt_ref[leaf] = own_features[:, leaf * LEAF : (leaf + 1) * LEAF].T

    pl.semaphore_wait(barrier, len(peers))

    gather_q.start(gather_q.first(0))
    def chunk(i):
        in_own, in_far = i < 4, i >= 12
        other = jnp.where(in_own, lax.div(i, 2), lax.rem(i, 2))
        core = lax.rem(place.core + other, 2)
        r = jnp.where(in_far, lax.div(i + 4, 2) - 8, jnp.where(in_own, 2 * lax.rem(i, 2), lax.div(i, 2) - 2))
        groups = (r, jnp.where(in_far, r + 2, jnp.where(in_own, r + 1, back(r))))
        planes = [jnp.where(in_far, 2, jnp.where(in_own, 0, p)) for p in (3, 1)]
        units = []
        for half in range(2):
            for unit in range(UNITS):
                part = max(unit - 1, 0)
                turn = lax.rem(part + core, 3)
                w = [pick3(turn, *((4, 1, 32) * 2)[s : s + 3]) for s in range(3)]
                u = place.along(turn)
                u2, u1 = lax.rem(u[2] + planes[half], SIDE), lax.rem(u[1] + groups[half], SIDE)
                device = core * 16 + u2 * w[2] + u1 * w[1]
                entry = core * (CORE_ROWS // LINES) + PART_BASE[part] // LINES
                size = PART_ROWS[part] // LINES
                entry = entry + (u2 * 16 + u1 * 4) * size + (unit % 2 if part == 0 else 0) * 2
                for u0 in range(SIDE):
                    units.append(((device + u0 * w[0]) * UNITS + unit, entry + u0 * size))
        return units

    def chunk_tile(i):
        columns = features(jnp.concatenate([x_ref[p] for p, _ in chunk(i)], axis=1), True).T
        return jnp.exp2(dot(columns, g_ref[...], ((1,), (0,)))).astype(bf16)

    def chunk_vectors(i):
        vectors = [jnp.concatenate([q_ref[v], q_ref[v + 1]], axis=0) for _, v in chunk(i)]
        return jnp.concatenate(vectors, axis=1)

    def early_tile(i, carry):
        @pl.when(i == 4)
        def _():
            gather_q.second()

        pre_ref[i] = chunk_tile(i)
        return carry

    lax.fori_loop(0, EARLY, early_tile, 0)
    gather_q.third()

    def arrive(i):
        even = lax.rem(i, 2) == 0

        @pl.when(i == 2)
        def _():
            gather_q.wait(gather_q.side_own())

        @pl.when((i >= 4) & (i < 12) & even)
        def _():
            gather_q.pass_near(lax.div(i, 2) - 2)

        @pl.when((i >= 4) & (i < 12) & jnp.logical_not(even))
        def _():
            gather_q.wait(gather_q.side_near(lax.div(i, 2) - 2))

        @pl.when((i >= 12) & even)
        def _():
            gather_q.pass_far(lax.div(i, 2) - 6)
            gather_q.pass_far(lax.div(i, 2) - 4)

        @pl.when((i >= 12) & jnp.logical_not(even))
        def _():
            gather_q.wait(gather_q.side_far(lax.div(i, 2) - 6))
            gather_q.wait(gather_q.side_far(lax.div(i, 2) - 4))

    def early_step(i, total):
        arrive(i)
        return total + dot(chunk_vectors(i), pre_ref[i], ((1,), (0,)))

    total = lax.fori_loop(0, EARLY, early_step, jnp.zeros((RANK, OWN), f32))

    def sketch_step(i, total):
        arrive(i)
        tile = chunk_tile(i)
        return total + dot(chunk_vectors(i), tile, ((1,), (0,)))

    narrow = lax.fori_loop(EARLY, 16, sketch_step, total)

    stacked = jnp.concatenate([narrow[:, :LEAF], narrow[:, LEAF:]], axis=0)
    left = lax.broadcasted_iota(jnp.int32, (1, 2 * RANK), 1) < RANK
    root, scale = inverse_root(stacked, left)
    scale = jnp.sqrt(scale)
    rounded = (dot(stacked, root, ((0,), (0,)), HIGHEST) / scale).astype(bf16)
    for unit, row in enumerate(gather_b.own_rows()):
        for n in range(2):
            at = unit * RANK + LINES * n
            b_ref[row + n] = rounded[at : at + LINES, :]
    gather_b.start(gather_b.first(0))

    packed = rounded.astype(f32)
    sc_ref[...] = packed
    flipped = packed.T
    for side in range(2):
        sct_ref[128 * side : 128 * (side + 1), :] = flipped[:, 128 * side : 128 * (side + 1)]
    even, odd = sc_ref[pl.ds(0, 128, stride=2), :], sc_ref[pl.ds(1, 128, stride=2), :]
    bases_out[0] = jnp.where(left, even, pltpu.roll(odd, RANK, 1)).astype(bf16)
    bases_out[1] = jnp.where(left, pltpu.roll(even, RANK, 1), odd).astype(bf16)
    half = RANK // 2
    for leaf in range(2):
        for odd_one in range(2):
            at = odd_one * half
            for side in range(2):
                first = 128 * side + leaf * RANK + odd_one
                bs_ref[leaf, at : at + half, 128 * side : 128 * (side + 1)] = sct_ref[
                    pl.ds(first, half, stride=2), :
                ].astype(bf16)

    def near_step(g, carry):
        @pl.when(g == 5)
        def _():
            gather_b.second()

        far = []
        for n in range(GROUP):
            entry = (owners[0, g * GROUP + n] * 2 + picks[1, g * GROUP + n]) * 2
            far += [x_ref[entry], x_ref[entry + 1]]
        far = features(jnp.concatenate(far, axis=1), True)
        tiles = []
        for n in range(GROUP):
            near_rows = gt_ref[picks[0, g * GROUP + n]]
            exponent = dot(near_rows, far[:, n * LEAF : (n + 1) * LEAF], ((1,), (0,)))
            tiles.append(jnp.exp2(exponent).astype(bf16))
        for n, tile in enumerate(tiles):
            k = g * GROUP + n
            l_ref[k] = dot(bs_ref[picks[0, k]], tile, ((1,), (0,))).astype(bf16)
        return carry

    lax.fori_loop(0, PAIRS // GROUP, near_step, 0)

    gather_b.third()

    def near_planes(r, carry):
        gather_b.pass_near(r)
        return carry

    def far_planes(r, carry):
        gather_b.pass_far(r)
        return carry

    def siblings(r, carry):
        gather_b.wait(gather_b.side_near(r))
        gather_b.wait(gather_b.side_far(r))
        return carry

    lax.fori_loop(0, 4, near_planes, 0)
    lax.fori_loop(0, 4, far_planes, 0)
    gather_b.wait(gather_b.side_own())
    lax.fori_loop(0, 4, siblings, 0)

    def far_step(g, carry):
        for pair in range(GROUP):
            k = g * GROUP + pair
            line, col = lax.div(owners[0, k], 16), lax.rem(owners[0, k], 16)
            core, z = lax.rem(line, 2), lax.div(line, 2)
            x, y = lax.div(col, SIDE), lax.rem(col, SIDE)
            slots = [z * 16 + y * 4 + x, x * 16 + z * 4 + y, y * 16 + x * 4 + z]
            blocks = []
            for part in range(3):
                slot = slots[part] + core * (slots[(part + 1) % 3] - slots[part])
                row = core * (CORE_ROWS // LINES) + PART_BASE[part] // LINES + slot * (PART_ROWS[part] // LINES)
                for n in range(PART_ROWS[part] // LINES):
                    blocks.append(b_ref[row + n])
            both = dot(
                l_ref[k],
                jnp.concatenate(blocks, axis=0),
                ((1,), (0,)),
            )
            even, odd = both[:half, :], both[half:, :]
            first = jnp.where(left, even, pltpu.roll(odd, RANK, 1))
            second = jnp.where(left, pltpu.roll(even, RANK, 1), odd)
            pick = picks[1, k].astype(f32)
            st_ref[pair * half : (pair + 1) * half, :] = first * (1.0 - pick) + second * pick
        rows = pl.ds(pl.multiple_of(g * GROUP, GROUP), GROUP)
        for i in range(half):
            coup_out[rows, 128 * i : 128 * (i + 1)] = st_ref[pl.ds(i, GROUP, stride=half), :]
        return carry

    lax.fori_loop(0, PAIRS // GROUP, far_step, 0)
    gather_q.finish_sends()
    gather_b.finish_sends()


def per_device(coords, panel, mixing, owners, leaf_picks):
    vmem = pl.BlockSpec(memory_space=pltpu.VMEM)
    smem = pl.BlockSpec(memory_space=pltpu.SMEM)
    sems = pltpu.SemaphoreType.DMA
    points = coords.shape[1]
    bases, couplings = pl.pallas_call(
        kernel,
        out_shape=(
            jax.ShapeDtypeStruct((2, 128, 128), bf16),
            jax.ShapeDtypeStruct((PAIRS, RANK * RANK), f32),
        ),
        in_specs=[pl.BlockSpec(memory_space=pl.ANY), vmem, vmem, smem, smem],
        out_specs=(vmem, vmem),
        scratch_shapes=[
            pltpu.VMEM((4, coords.shape[0], points // INPUTS), f32),
            pltpu.VMEM((points // UNIT, coords.shape[0], UNIT), f32),
            pltpu.VMEM((EARLY, CHUNK, OWN), bf16),
            pltpu.VMEM((2 * CORE_ROWS // LINES, LINES, 128), bf16),
            pltpu.VMEM((2 * CORE_ROWS // LINES, LINES, 128), bf16),
            pltpu.VMEM((128, OWN), bf16),
            pltpu.VMEM((2, LEAF, 128), bf16),
            pltpu.VMEM((PAIRS, RANK, LEAF), bf16),
            pltpu.VMEM((2, RANK, LEAF), bf16),
            pltpu.VMEM((LEAF, 128), f32),
            pltpu.VMEM((2 * 128, 128), f32),
            pltpu.VMEM((GROUP * RANK // 2, 128), f32),
            sems((4,)),
            sems((3, 18)),
            sems((3, 18)),
            sems((3, 13)),
            sems((3, 13)),
            sems((3, 18)),
            sems((3, 18)),
            sems((3, 13)),
            sems((3, 13)),
        ],
        compiler_params=pltpu.CompilerParams(
            collective_id=0, has_side_effects=True, vmem_limit_bytes=60 * 2**20
        ),
    )(coords, panel, mixing.T, owners.T, leaf_picks.T)
    return bases.reshape(2, LEAF * RANK), couplings


def solution(mesh):
    return jax.shard_map(
        per_device,
        mesh=mesh,
        in_specs=(
            P(),
            P(("row", "col"), None),
            P(),
            P(("row", "col"), None),
            P(("row", "col"), None),
        ),
        out_specs=(P(("row", "col"), None), P(("row", "col"), None)),
        check_vma=False,
    )
```

```python
import functools
import math

import jax
import jax.numpy as jnp
from jax import lax
from jax.experimental import pallas as pl
from jax.experimental.pallas import tpu as pltpu
from jax.sharding import PartitionSpec as P

MESH = pl.DeviceIdType.MESH
HIGHEST = lax.Precision.HIGHEST
f32, bf16 = jnp.float32, jnp.bfloat16

LEAF = 256
RANK = 64
NSWEEPS = 6
EPSILON = 1e-06
OWN = 512
UNIT = 128
UNITS = 4
PAIRS = 64
GROUP = 8
LINES = 32
SIDE = 4
CHUNK = 4096
EARLY = 6
INPUTS = 16
PART_UNITS = (2, 1, 1)
PART_ROWS = tuple(RANK * u for u in PART_UNITS)
PART_BASE = (0, 128 * SIDE**3, 192 * SIDE**3)
CORE_ROWS = 256 * SIDE**3


def dot(a, b, dims, precision=None):
    return lax.dot_general(
        a, b, (dims, ((), ())), precision=precision, preferred_element_type=f32
    )


def pick3(k, a, b, c):
    return jnp.where(k == 0, a, jnp.where(k == 1, b, c))


def back(j):
    return jnp.where(j == 0, 0, lax.rem(j, 3) + 1)


def split3(v):
    hi = v.astype(bf16)
    rest = v - hi.astype(f32)
    mid = rest.astype(bf16)
    lo = (rest - mid.astype(f32)).astype(bf16)
    return hi, mid, lo


def features(x, column):
    n = x.shape[1]
    a = x * math.sqrt(4.0 * math.log2(math.e) / x.shape[0])
    h = -0.5 * jnp.sum(a * a, axis=0, keepdims=True)
    hi, mid, lo = split3(a)
    parts = [jnp.broadcast_to(v.astype(f32), (16, n)) for v in split3(h)]
    line = lax.broadcasted_iota(jnp.int32, (16, n), 0)
    at = 0 if column else 3
    extra = jnp.where(line < 6, 1.0, 0.0)
    for k in range(3):
        extra = jnp.where(line == at + k, parts[k], extra)
    extra = extra.astype(bf16)
    zero = jnp.zeros((16, n), bf16)
    if column:
        stack = [hi, hi, mid, mid, hi, lo, extra, zero]
    else:
        stack = [hi, mid, hi, mid, lo, hi, extra, zero]
    return jnp.concatenate(stack, axis=0)


class Place:
    def __init__(self):
        row, col = lax.axis_index("row"), lax.axis_index("col")
        self.core = lax.rem(row, 2)
        self.z = lax.div(row, 2)
        self.x = lax.div(col, SIDE)
        self.y = lax.rem(col, SIDE)
        self.index = row * SIDE * SIDE + col

    def sibling(self):
        return (self.z * 2 + 1 - self.core, self.x * SIDE + self.y)

    def neighbour(self, axis, step):
        x = lax.rem(self.x + jnp.where(axis == 0, step, 0), SIDE)
        y = lax.rem(self.y + jnp.where(axis == 1, step, 0), SIDE)
        z = lax.rem(self.z + jnp.where(axis == 2, step, 0), SIDE)
        return (z * 2 + self.core, x * SIDE + y)

    def along(self, turn):
        c = (self.x, self.y, self.z)
        return [pick3(turn, c[s], c[(s + 1) % 3], c[(s + 2) % 3]) for s in range(3)]


class Gather:
    def __init__(self, place, buf, send, recv, sib_send, sib_recv):
        self.place, self.buf = place, buf
        self.send, self.recv = send, recv
        self.sib_send, self.sib_recv = sib_send, sib_recv

    def turn(self, part):
        return lax.rem(part + self.place.core, 3)

    def start_row(self, part, slot):
        return self.place.core * CORE_ROWS + PART_BASE[part] + slot * PART_ROWS[part]

    def ref(self, part, plane, group, slot, slots):
        first = lax.rem(plane, SIDE) * 16 + lax.rem(group, SIDE) * 4 + slot
        start = lax.div(self.start_row(part, first), LINES)
        return self.buf.at[pl.ds(start, slots * PART_ROWS[part] // LINES)]

    def copy(self, part, stage, ref, step, sem):
        return pltpu.make_async_remote_copy(
            src_ref=ref,
            dst_ref=ref,
            send_sem=self.send.at[part, sem],
            recv_sem=self.recv.at[part, sem],
            device_id=self.place.neighbour(lax.rem(self.turn(part) + stage, 3), step),
            device_id_type=MESH,
        )

    def first(self, stage):
        result = []
        for part in range(3):
            u = self.place.along(self.turn(part))
            ref = self.ref(part, u[2], u[1], u[0] if stage == 0 else 0, 1 if stage == 0 else 4)
            result += [self.copy(part, stage, ref, s, 3 * stage + s - 1) for s in (1, 2, 3)]
        return result

    def near_plane(self, j):
        result = []
        for part in range(3):
            u = self.place.along(self.turn(part))
            for way, (r, s) in enumerate(((j, 1), (back(j), SIDE - 1))):
                ref = self.ref(part, u[2], u[1] + r, 0, 4)
                result.append(self.copy(part, 2, ref, s, 6 + 2 * j + way))
        return result

    def far_plane(self, r):
        step = 1 + 2 * lax.div(r, 2)
        result = []
        for part in range(3):
            u = self.place.along(self.turn(part))
            ref = self.ref(part, u[2] + SIDE - step, u[1] + r, 0, 4)
            result.append(self.copy(part, 2, ref, step, 14 + r))
        return result

    def side(self, ref, part, sem):
        return pltpu.make_async_remote_copy(
            src_ref=ref,
            dst_ref=ref,
            send_sem=self.sib_send.at[part, sem],
            recv_sem=self.sib_recv.at[part, sem],
            device_id=self.place.sibling(),
            device_id_type=MESH,
        )

    def side_own(self):
        result = []
        for part in range(3):
            u = self.place.along(self.turn(part))
            result.append(self.side(self.ref(part, u[2], 0, 0, 16), part, 0))
        return result

    def side_near(self, j):
        result = []
        for part in range(3):
            u = self.place.along(self.turn(part))
            for way, (r, plane) in enumerate(((j, 3), (back(j), 1))):
                ref = self.ref(part, u[2] + plane, u[1] + r, 0, 4)
                result.append(self.side(ref, part, 1 + 2 * j + way))
        return result

    def side_far(self, r):
        result = []
        for part in range(3):
            u = self.place.along(self.turn(part))
            result.append(self.side(self.ref(part, u[2] + 2, u[1] + r, 0, 4), part, 9 + r))
        return result

    def start(self, copies):
        for copy in copies:
            copy.start()

    def wait(self, copies):
        for copy in copies:
            copy.wait_recv()

    def second(self):
        self.wait(self.first(0))
        self.start(self.first(1))
        self.start(self.near_plane(0))

    def third(self):
        self.wait(self.first(1))
        for r in range(1, 4):
            self.start(self.near_plane(r))
        self.start(self.side_own())

    def pass_near(self, j):
        self.wait(self.near_plane(j))
        for r, when in enumerate((0, 1, 1, 2)):

            @pl.when(j == when)
            def _(r=r):
                self.start(self.far_plane(r))

        self.start(self.side_near(j))

    def pass_far(self, r):
        self.wait(self.far_plane(r))
        self.start(self.side_far(r))

    def own_rows(self):
        rows = []
        for part in range(3):
            u = self.place.along(self.turn(part))
            start = self.start_row(part, u[2] * 16 + u[1] * 4 + u[0])
            for unit in range(PART_UNITS[part]):
                rows.append(lax.div(start + unit * RANK, LINES))
        return rows

    def finish_sends(self):
        for copy in self.first(0) + self.first(1) + self.side_own():
            copy.wait_send()

        def step(r, carry):
            copies = self.near_plane(r) + self.far_plane(r) + self.side_near(r) + self.side_far(r)
            for copy in copies:
                copy.wait_send()
            return carry

        lax.fori_loop(0, 4, step, 0)


def dot3(a, b):
    ah, bh = a.astype(bf16), b.astype(bf16)
    al, bl = (a - ah.astype(f32)).astype(bf16), (b - bh.astype(f32)).astype(bf16)
    by = ((1,), (0,))
    return dot(ah, bh, by) + (dot(ah, bl, by) + dot(al, bh, by))


def inverse_root(stacked, left):
    shape = (2 * RANK, 2 * RANK)
    row = lax.broadcasted_iota(jnp.int32, shape, 0)
    col = lax.broadcasted_iota(jnp.int32, shape, 1)
    gram = jnp.where((row < RANK) == (col < RANK), dot(stacked, stacked, ((1,), (1,)), HIGHEST), 0.0)
    sums = jnp.sum(gram * gram, axis=0, keepdims=True)
    zero = jnp.zeros_like(sums)
    sums = [jnp.sum(v, axis=1, keepdims=True) for v in (jnp.where(left, sums, zero), jnp.where(left, zero, sums))]
    scale = jnp.sqrt(jnp.where(left, sums[0], sums[1]) + EPSILON)
    iterate = gram / scale
    ident = jnp.where(row == col, 1.0, 0.0)
    root = ident
    for sweep in range(NSWEEPS):
        product = iterate if sweep == 0 else dot3(root, iterate)
        factor = 1.5 * ident - 0.5 * product
        if sweep < NSWEEPS - 1:
            iterate = dot3(iterate, factor)
        root = factor if sweep == 0 else dot3(factor, root)
    return root, scale


def kernel(
    coords, panel, mixing, owners, picks, bases_out, coup_out,
    in_ref, x_ref, pre_ref, q_ref, b_ref, g_ref, gt_ref, l_ref, bs_ref, sc_ref, sct_ref, st_ref,
    in_sem, q_send, q_recv, q_sib_send, q_sib_recv, b_send, b_recv, b_sib_send, b_sib_recv,
):
    place = Place()
    gather_q = Gather(place, q_ref, q_send, q_recv, q_sib_send, q_sib_recv)
    gather_b = Gather(place, b_ref, b_send, b_recv, b_sib_send, b_sib_recv)

    width = coords.shape[1] // INPUTS

    def load(j):
        return pltpu.make_async_copy(
            coords.at[:, j * width : (j + 1) * width], in_ref.at[j % 4], in_sem.at[j % 4]
        )

    for j in range(4):
        load(j).start()
    barrier = pltpu.get_barrier_semaphore()
    peers = [place.neighbour(axis, step) for axis in range(3) for step in (1, 2, 3)]
    peers.append(place.sibling())
    for peer in peers:
        pl.semaphore_signal(barrier, inc=1, device_id=peer, device_id_type=MESH)

    vectors = dot(mixing[...], panel[...].astype(f32), ((1,), (1,)), HIGHEST).astype(bf16)
    for unit, row in enumerate(gather_q.own_rows()):
        for n in range(2):
            q_ref[row + n] = vectors[LINES * n : LINES * (n + 1), unit * UNIT : (unit + 1) * UNIT]
    for j in range(INPUTS):
        load(j).wait()
        for unit in range(width // UNIT):
            x_ref[j * width // UNIT + unit] = in_ref[j % 4, :, unit * UNIT : (unit + 1) * UNIT]
        if j + 4 < INPUTS:
            load(j + 4).start()
    own = [x_ref[place.index * UNITS + unit] for unit in range(UNITS)]
    own_features = features(jnp.concatenate(own, axis=1), False)
    g_ref[...] = own_features
    for leaf in range(2):
        gt_ref[leaf] = own_features[:, leaf * LEAF : (leaf + 1) * LEAF].T

    pl.semaphore_wait(barrier, len(peers))

    gather_q.start(gather_q.first(0))
    def chunk(i):
        in_own, in_far = i < 4, i >= 12
        other = jnp.where(in_own, lax.div(i, 2), lax.rem(i, 2))
        core = lax.rem(place.core + other, 2)
        r = jnp.where(in_far, lax.div(i + 4, 2) - 8, jnp.where(in_own, 2 * lax.rem(i, 2), lax.div(i, 2) - 2))
        groups = (r, jnp.where(in_far, r + 2, jnp.where(in_own, r + 1, back(r))))
        planes = [jnp.where(in_far, 2, jnp.where(in_own, 0, p)) for p in (3, 1)]
        units = []
        for half in range(2):
            for unit in range(UNITS):
                part = max(unit - 1, 0)
                turn = lax.rem(part + core, 3)
                w = [pick3(turn, *((4, 1, 32) * 2)[s : s + 3]) for s in range(3)]
                u = place.along(turn)
                u2, u1 = lax.rem(u[2] + planes[half], SIDE), lax.rem(u[1] + groups[half], SIDE)
                device = core * 16 + u2 * w[2] + u1 * w[1]
                entry = core * (CORE_ROWS // LINES) + PART_BASE[part] // LINES
                size = PART_ROWS[part] // LINES
                entry = entry + (u2 * 16 + u1 * 4) * size + (unit % 2 if part == 0 else 0) * 2
                for u0 in range(SIDE):
                    units.append(((device + u0 * w[0]) * UNITS + unit, entry + u0 * size))
        return units

    def chunk_tile(i):
        columns = features(jnp.concatenate([x_ref[p] for p, _ in chunk(i)], axis=1), True).T
        return jnp.exp2(dot(columns, g_ref[...], ((1,), (0,)))).astype(bf16)

    def chunk_vectors(i):
        vectors = [jnp.concatenate([q_ref[v], q_ref[v + 1]], axis=0) for _, v in chunk(i)]
        return jnp.concatenate(vectors, axis=1)

    def early_tile(i, carry):
        @pl.when(i == 4)
        def _():
            gather_q.second()

        pre_ref[i] = chunk_tile(i)
        return carry

    lax.fori_loop(0, EARLY, early_tile, 0)
    gather_q.third()

    def arrive(i):
        even = lax.rem(i, 2) == 0

        @pl.when(i == 2)
        def _():
            gather_q.wait(gather_q.side_own())

        @pl.when((i >= 4) & (i < 12) & even)
        def _():
            gather_q.pass_near(lax.div(i, 2) - 2)

        @pl.when((i >= 4) & (i < 12) & jnp.logical_not(even))
        def _():
            gather_q.wait(gather_q.side_near(lax.div(i, 2) - 2))

        @pl.when((i >= 12) & even)
        def _():
            gather_q.pass_far(lax.div(i, 2) - 6)
            gather_q.pass_far(lax.div(i, 2) - 4)

        @pl.when((i >= 12) & jnp.logical_not(even))
        def _():
            gather_q.wait(gather_q.side_far(lax.div(i, 2) - 6))
            gather_q.wait(gather_q.side_far(lax.div(i, 2) - 4))

    def early_step(i, total):
        arrive(i)
        return total + dot(chunk_vectors(i), pre_ref[i], ((1,), (0,)))

    total = lax.fori_loop(0, EARLY, early_step, jnp.zeros((RANK, OWN), f32))

    def sketch_step(i, total):
        arrive(i)
        tile = chunk_tile(i)
        return total + dot(chunk_vectors(i), tile, ((1,), (0,)))

    narrow = lax.fori_loop(EARLY, 16, sketch_step, total)

    stacked = jnp.concatenate([narrow[:, :LEAF], narrow[:, LEAF:]], axis=0)
    left = lax.broadcasted_iota(jnp.int32, (1, 2 * RANK), 1) < RANK
    root, scale = inverse_root(stacked, left)
    scale = jnp.sqrt(scale)
    rounded = (dot(stacked, root, ((0,), (0,)), HIGHEST) / scale).astype(bf16)
    for unit, row in enumerate(gather_b.own_rows()):
        for n in range(2):
            at = unit * RANK + LINES * n
            b_ref[row + n] = rounded[at : at + LINES, :]
    gather_b.start(gather_b.first(0))

    packed = rounded.astype(f32)
    sc_ref[...] = packed
    flipped = packed.T
    for side in range(2):
        sct_ref[128 * side : 128 * (side + 1), :] = flipped[:, 128 * side : 128 * (side + 1)]
    even, odd = sc_ref[pl.ds(0, 128, stride=2), :], sc_ref[pl.ds(1, 128, stride=2), :]
    sc_ref[:128, :] = jnp.where(left, even, pltpu.roll(odd, RANK, 1))
    sc_ref[128:, :] = jnp.where(left, pltpu.roll(even, RANK, 1), odd)
    for i in range(128):
        bases_out[:, 128 * i : 128 * (i + 1)] = sc_ref[pl.ds(i, 2, stride=128), :].astype(bf16)
    half = RANK // 2
    for leaf in range(2):
        for odd_one in range(2):
            at = odd_one * half
            for side in range(2):
                first = 128 * side + leaf * RANK + odd_one
                bs_ref[leaf, at : at + half, 128 * side : 128 * (side + 1)] = sct_ref[
                    pl.ds(first, half, stride=2), :
                ].astype(bf16)

    def near_step(g, carry):
        @pl.when(g == 5)
        def _():
            gather_b.second()

        far = []
        for n in range(GROUP):
            entry = (owners[0, g * GROUP + n] * 2 + picks[1, g * GROUP + n]) * 2
            far += [x_ref[entry], x_ref[entry + 1]]
        far = features(jnp.concatenate(far, axis=1), True)
        tiles = []
        for n in range(GROUP):
            near_rows = gt_ref[picks[0, g * GROUP + n]]
            exponent = dot(near_rows, far[:, n * LEAF : (n + 1) * LEAF], ((1,), (0,)))
            tiles.append(jnp.exp2(exponent).astype(bf16))
        for n, tile in enumerate(tiles):
            k = g * GROUP + n
            l_ref[k] = dot(bs_ref[picks[0, k]], tile, ((1,), (0,))).astype(bf16)
        return carry

    lax.fori_loop(0, PAIRS // GROUP, near_step, 0)

    gather_b.third()

    def near_planes(r, carry):
        gather_b.pass_near(r)
        return carry

    def far_planes(r, carry):
        gather_b.pass_far(r)
        return carry

    def siblings(r, carry):
        gather_b.wait(gather_b.side_near(r))
        gather_b.wait(gather_b.side_far(r))
        return carry

    lax.fori_loop(0, 4, near_planes, 0)
    lax.fori_loop(0, 4, far_planes, 0)
    gather_b.wait(gather_b.side_own())
    lax.fori_loop(0, 4, siblings, 0)

    def far_step(g, carry):
        for pair in range(GROUP):
            k = g * GROUP + pair
            line, col = lax.div(owners[0, k], 16), lax.rem(owners[0, k], 16)
            core, z = lax.rem(line, 2), lax.div(line, 2)
            x, y = lax.div(col, SIDE), lax.rem(col, SIDE)
            slots = [z * 16 + y * 4 + x, x * 16 + z * 4 + y, y * 16 + x * 4 + z]
            blocks = []
            for part in range(3):
                slot = slots[part] + core * (slots[(part + 1) % 3] - slots[part])
                row = core * (CORE_ROWS // LINES) + PART_BASE[part] // LINES + slot * (PART_ROWS[part] // LINES)
                for n in range(PART_ROWS[part] // LINES):
                    blocks.append(b_ref[row + n])
            both = dot(
                l_ref[k],
                jnp.concatenate(blocks, axis=0),
                ((1,), (0,)),
            )
            even, odd = both[:half, :], both[half:, :]
            first = jnp.where(left, even, pltpu.roll(odd, RANK, 1))
            second = jnp.where(left, pltpu.roll(even, RANK, 1), odd)
            pick = picks[1, k].astype(f32)
            st_ref[pair * half : (pair + 1) * half, :] = first * (1.0 - pick) + second * pick
        rows = pl.ds(pl.multiple_of(g * GROUP, GROUP), GROUP)
        for i in range(half):
            coup_out[rows, 128 * i : 128 * (i + 1)] = st_ref[pl.ds(i, GROUP, stride=half), :]
        return carry

    lax.fori_loop(0, PAIRS // GROUP, far_step, 0)
    gather_q.finish_sends()
    gather_b.finish_sends()


def per_device(coords, panel, mixing, owners, leaf_picks):
    vmem = pl.BlockSpec(memory_space=pltpu.VMEM)
    smem = pl.BlockSpec(memory_space=pltpu.SMEM)
    sems = pltpu.SemaphoreType.DMA
    points = coords.shape[1]
    bases, couplings = pl.pallas_call(
        kernel,
        out_shape=(
            pltpu.VMEM((2, LEAF * RANK), bf16),
            pltpu.VMEM((PAIRS, RANK * RANK), f32),
        ),
        in_specs=[pl.BlockSpec(memory_space=pl.ANY), vmem, vmem, smem, smem],
        out_specs=(vmem, vmem),
        scratch_shapes=[
            pltpu.VMEM((4, coords.shape[0], points // INPUTS), f32),
            pltpu.VMEM((points // UNIT, coords.shape[0], UNIT), f32),
            pltpu.VMEM((EARLY, CHUNK, OWN), bf16),
            pltpu.VMEM((2 * CORE_ROWS // LINES, LINES, 128), bf16),
            pltpu.VMEM((2 * CORE_ROWS // LINES, LINES, 128), bf16),
            pltpu.VMEM((128, OWN), bf16),
            pltpu.VMEM((2, LEAF, 128), bf16),
            pltpu.VMEM((PAIRS, RANK, LEAF), bf16),
            pltpu.VMEM((2, RANK, LEAF), bf16),
            pltpu.VMEM((LEAF, 128), f32),
            pltpu.VMEM((2 * 128, 128), f32),
            pltpu.VMEM((GROUP * RANK // 2, 128), f32),
            sems((4,)),
            sems((3, 18)),
            sems((3, 18)),
            sems((3, 13)),
            sems((3, 13)),
            sems((3, 18)),
            sems((3, 18)),
            sems((3, 13)),
            sems((3, 13)),
        ],
        compiler_params=pltpu.CompilerParams(
            collective_id=0, has_side_effects=True, vmem_limit_bytes=60 * 2**20
        ),
    )(coords, panel, mixing.T, owners.T, leaf_picks.T)
    return bases, couplings


def solution(mesh):
    return jax.shard_map(
        per_device,
        mesh=mesh,
        in_specs=(
            P(),
            P(("row", "col"), None),
            P(),
            P(("row", "col"), None),
            P(("row", "col"), None),
        ),
        out_specs=(P(("row", "col"), None), P(("row", "col"), None)),
        check_vma=False,
    )
```

```python
import functools
import math

import jax
import jax.numpy as jnp
from jax import lax
from jax.experimental import pallas as pl
from jax.experimental.pallas import tpu as pltpu
from jax.sharding import PartitionSpec as P

MESH = pl.DeviceIdType.MESH
HIGHEST = lax.Precision.HIGHEST
f32, bf16 = jnp.float32, jnp.bfloat16

LEAF = 256
RANK = 64
NSWEEPS = 6
EPSILON = 1e-06
OWN = 512
UNIT = 128
UNITS = 4
PAIRS = 64
GROUP = 8
LINES = 32
SIDE = 4
CHUNK = 4096
EARLY = 7
INPUTS = 16
PART_UNITS = (2, 1, 1)
PART_ROWS = tuple(RANK * u for u in PART_UNITS)
PART_BASE = (0, 128 * SIDE**3, 192 * SIDE**3)
CORE_ROWS = 256 * SIDE**3


def dot(a, b, dims, precision=None):
    return lax.dot_general(
        a, b, (dims, ((), ())), precision=precision, preferred_element_type=f32
    )


def pick3(k, a, b, c):
    return jnp.where(k == 0, a, jnp.where(k == 1, b, c))


def back(j):
    return jnp.where(j == 0, 0, lax.rem(j, 3) + 1)


def split3(v):
    hi = v.astype(bf16)
    rest = v - hi.astype(f32)
    mid = rest.astype(bf16)
    lo = (rest - mid.astype(f32)).astype(bf16)
    return hi, mid, lo


def features(x, column):
    n = x.shape[1]
    a = x * math.sqrt(4.0 * math.log2(math.e) / x.shape[0])
    h = -0.5 * jnp.sum(a * a, axis=0, keepdims=True)
    hi, mid, lo = split3(a)
    parts = [jnp.broadcast_to(v.astype(f32), (16, n)) for v in split3(h)]
    line = lax.broadcasted_iota(jnp.int32, (16, n), 0)
    at = 0 if column else 3
    extra = jnp.where(line < 6, 1.0, 0.0)
    for k in range(3):
        extra = jnp.where(line == at + k, parts[k], extra)
    extra = extra.astype(bf16)
    zero = jnp.zeros((16, n), bf16)
    if column:
        stack = [hi, hi, mid, mid, hi, lo, extra, zero]
    else:
        stack = [hi, mid, hi, mid, lo, hi, extra, zero]
    return jnp.concatenate(stack, axis=0)


class Place:
    def __init__(self):
        row, col = lax.axis_index("row"), lax.axis_index("col")
        self.core = lax.rem(row, 2)
        self.z = lax.div(row, 2)
        self.x = lax.div(col, SIDE)
        self.y = lax.rem(col, SIDE)
        self.index = row * SIDE * SIDE + col

    def sibling(self):
        return (self.z * 2 + 1 - self.core, self.x * SIDE + self.y)

    def neighbour(self, axis, step):
        x = lax.rem(self.x + jnp.where(axis == 0, step, 0), SIDE)
        y = lax.rem(self.y + jnp.where(axis == 1, step, 0), SIDE)
        z = lax.rem(self.z + jnp.where(axis == 2, step, 0), SIDE)
        return (z * 2 + self.core, x * SIDE + y)

    def along(self, turn):
        c = (self.x, self.y, self.z)
        return [pick3(turn, c[s], c[(s + 1) % 3], c[(s + 2) % 3]) for s in range(3)]


class Gather:
    def __init__(self, place, buf, send, recv, sib_send, sib_recv):
        self.place, self.buf = place, buf
        self.send, self.recv = send, recv
        self.sib_send, self.sib_recv = sib_send, sib_recv

    def turn(self, part):
        return lax.rem(part + self.place.core, 3)

    def start_row(self, part, slot):
        return self.place.core * CORE_ROWS + PART_BASE[part] + slot * PART_ROWS[part]

    def ref(self, part, plane, group, slot, slots):
        first = lax.rem(plane, SIDE) * 16 + lax.rem(group, SIDE) * 4 + slot
        start = lax.div(self.start_row(part, first), LINES)
        return self.buf.at[pl.ds(start, slots * PART_ROWS[part] // LINES)]

    def copy(self, part, stage, ref, step, sem):
        return pltpu.make_async_remote_copy(
            src_ref=ref,
            dst_ref=ref,
            send_sem=self.send.at[part, sem],
            recv_sem=self.recv.at[part, sem],
            device_id=self.place.neighbour(lax.rem(self.turn(part) + stage, 3), step),
            device_id_type=MESH,
        )

    def first(self, stage):
        result = []
        for part in range(3):
            u = self.place.along(self.turn(part))
            ref = self.ref(part, u[2], u[1], u[0] if stage == 0 else 0, 1 if stage == 0 else 4)
            result += [self.copy(part, stage, ref, s, 3 * stage + s - 1) for s in (1, 2, 3)]
        return result

    def near_plane(self, j):
        result = []
        for part in range(3):
            u = self.place.along(self.turn(part))
            for way, (r, s) in enumerate(((j, 1), (back(j), SIDE - 1))):
                ref = self.ref(part, u[2], u[1] + r, 0, 4)
                result.append(self.copy(part, 2, ref, s, 6 + 2 * j + way))
        return result

    def far_plane(self, r):
        step = 1 + 2 * lax.div(r, 2)
        result = []
        for part in range(3):
            u = self.place.along(self.turn(part))
            ref = self.ref(part, u[2] + SIDE - step, u[1] + r, 0, 4)
            result.append(self.copy(part, 2, ref, step, 14 + r))
        return result

    def side(self, ref, part, sem):
        return pltpu.make_async_remote_copy(
            src_ref=ref,
            dst_ref=ref,
            send_sem=self.sib_send.at[part, sem],
            recv_sem=self.sib_recv.at[part, sem],
            device_id=self.place.sibling(),
            device_id_type=MESH,
        )

    def side_own(self):
        result = []
        for part in range(3):
            u = self.place.along(self.turn(part))
            result.append(self.side(self.ref(part, u[2], 0, 0, 16), part, 0))
        return result

    def side_near(self, j):
        result = []
        for part in range(3):
            u = self.place.along(self.turn(part))
            for way, (r, plane) in enumerate(((j, 3), (back(j), 1))):
                ref = self.ref(part, u[2] + plane, u[1] + r, 0, 4)
                result.append(self.side(ref, part, 1 + 2 * j + way))
        return result

    def side_far(self, r):
        result = []
        for part in range(3):
            u = self.place.along(self.turn(part))
            result.append(self.side(self.ref(part, u[2] + 2, u[1] + r, 0, 4), part, 9 + r))
        return result

    def start(self, copies):
        for copy in copies:
            copy.start()

    def wait(self, copies):
        for copy in copies:
            copy.wait_recv()

    def second(self):
        self.wait(self.first(0))
        self.start(self.first(1))
        self.start(self.near_plane(0))

    def third(self):
        self.wait(self.first(1))
        for r in range(1, 4):
            self.start(self.near_plane(r))
        self.start(self.side_own())

    def pass_near(self, j):
        self.wait(self.near_plane(j))
        for r, when in enumerate((0, 1, 1, 2)):

            @pl.when(j == when)
            def _(r=r):
                self.start(self.far_plane(r))

        self.start(self.side_near(j))

    def pass_far(self, r):
        self.wait(self.far_plane(r))
        self.start(self.side_far(r))

    def own_rows(self):
        rows = []
        for part in range(3):
            u = self.place.along(self.turn(part))
            start = self.start_row(part, u[2] * 16 + u[1] * 4 + u[0])
            for unit in range(PART_UNITS[part]):
                rows.append(lax.div(start + unit * RANK, LINES))
        return rows

    def finish_sends(self):
        for copy in self.first(0) + self.first(1) + self.side_own():
            copy.wait_send()

        def step(r, carry):
            copies = self.near_plane(r) + self.far_plane(r) + self.side_near(r) + self.side_far(r)
            for copy in copies:
                copy.wait_send()
            return carry

        lax.fori_loop(0, 4, step, 0)


def dot3(a, b):
    ah, bh = a.astype(bf16), b.astype(bf16)
    al, bl = (a - ah.astype(f32)).astype(bf16), (b - bh.astype(f32)).astype(bf16)
    by = ((1,), (0,))
    return dot(ah, bh, by) + (dot(ah, bl, by) + dot(al, bh, by))


def inverse_root(stacked, left):
    shape = (2 * RANK, 2 * RANK)
    row = lax.broadcasted_iota(jnp.int32, shape, 0)
    col = lax.broadcasted_iota(jnp.int32, shape, 1)
    gram = jnp.where((row < RANK) == (col < RANK), dot(stacked, stacked, ((1,), (1,)), HIGHEST), 0.0)
    sums = jnp.sum(gram * gram, axis=0, keepdims=True)
    zero = jnp.zeros_like(sums)
    sums = [jnp.sum(v, axis=1, keepdims=True) for v in (jnp.where(left, sums, zero), jnp.where(left, zero, sums))]
    scale = jnp.sqrt(jnp.where(left, sums[0], sums[1]) + EPSILON)
    iterate = gram / scale
    ident = jnp.where(row == col, 1.0, 0.0)
    root = ident
    for sweep in range(NSWEEPS):
        product = iterate if sweep == 0 else dot3(root, iterate)
        factor = 1.5 * ident - 0.5 * product
        if sweep < NSWEEPS - 1:
            iterate = dot3(iterate, factor)
        root = factor if sweep == 0 else dot3(factor, root)
    return root, scale


def kernel(
    coords, panel, mixing, owners, picks, bases_out, coup_out,
    in_ref, x_ref, pre_ref, q_ref, b_ref, g_ref, gt_ref, bs_ref, sc_ref, sct_ref, st_ref,
    in_sem, q_send, q_recv, q_sib_send, q_sib_recv, b_send, b_recv, b_sib_send, b_sib_recv,
):
    place = Place()
    gather_q = Gather(place, q_ref, q_send, q_recv, q_sib_send, q_sib_recv)
    gather_b = Gather(place, b_ref, b_send, b_recv, b_sib_send, b_sib_recv)

    width = coords.shape[1] // INPUTS

    def load(j):
        return pltpu.make_async_copy(
            coords.at[:, j * width : (j + 1) * width], in_ref.at[j % 4], in_sem.at[j % 4]
        )

    for j in range(4):
        load(j).start()
    barrier = pltpu.get_barrier_semaphore()
    peers = [place.neighbour(axis, step) for axis in range(3) for step in (1, 2, 3)]
    peers.append(place.sibling())
    for peer in peers:
        pl.semaphore_signal(barrier, inc=1, device_id=peer, device_id_type=MESH)

    vectors = dot(mixing[...], panel[...].astype(f32), ((1,), (1,)), HIGHEST).astype(bf16)
    for unit, row in enumerate(gather_q.own_rows()):
        for n in range(2):
            q_ref[row + n] = vectors[LINES * n : LINES * (n + 1), unit * UNIT : (unit + 1) * UNIT]
    for j in range(INPUTS):
        load(j).wait()
        for unit in range(width // UNIT):
            x_ref[j * width // UNIT + unit] = in_ref[j % 4, :, unit * UNIT : (unit + 1) * UNIT]
        if j + 4 < INPUTS:
            load(j + 4).start()
    own = [x_ref[place.index * UNITS + unit] for unit in range(UNITS)]
    own_features = features(jnp.concatenate(own, axis=1), False)
    g_ref[...] = own_features
    for leaf in range(2):
        gt_ref[leaf] = own_features[:, leaf * LEAF : (leaf + 1) * LEAF].T

    pl.semaphore_wait(barrier, len(peers))

    gather_q.start(gather_q.first(0))
    def chunk(i):
        in_own, in_far = i < 4, i >= 12
        other = jnp.where(in_own, lax.div(i, 2), lax.rem(i, 2))
        core = lax.rem(place.core + other, 2)
        r = jnp.where(in_far, lax.div(i + 4, 2) - 8, jnp.where(in_own, 2 * lax.rem(i, 2), lax.div(i, 2) - 2))
        groups = (r, jnp.where(in_far, r + 2, jnp.where(in_own, r + 1, back(r))))
        planes = [jnp.where(in_far, 2, jnp.where(in_own, 0, p)) for p in (3, 1)]
        units = []
        for half in range(2):
            for unit in range(UNITS):
                part = max(unit - 1, 0)
                turn = lax.rem(part + core, 3)
                w = [pick3(turn, *((4, 1, 32) * 2)[s : s + 3]) for s in range(3)]
                u = place.along(turn)
                u2, u1 = lax.rem(u[2] + planes[half], SIDE), lax.rem(u[1] + groups[half], SIDE)
                device = core * 16 + u2 * w[2] + u1 * w[1]
                entry = core * (CORE_ROWS // LINES) + PART_BASE[part] // LINES
                size = PART_ROWS[part] // LINES
                entry = entry + (u2 * 16 + u1 * 4) * size + (unit % 2 if part == 0 else 0) * 2
                for u0 in range(SIDE):
                    units.append(((device + u0 * w[0]) * UNITS + unit, entry + u0 * size))
        return units

    def chunk_tile(i):
        columns = features(jnp.concatenate([x_ref[p] for p, _ in chunk(i)], axis=1), True).T
        return jnp.exp2(dot(columns, g_ref[...], ((1,), (0,)))).astype(bf16)

    def chunk_vectors(i):
        vectors = [jnp.concatenate([q_ref[v], q_ref[v + 1]], axis=0) for _, v in chunk(i)]
        return jnp.concatenate(vectors, axis=1)

    def early_tile(i, carry):
        @pl.when(i == 4)
        def _():
            gather_q.second()

        pre_ref[i] = chunk_tile(i)
        return carry

    lax.fori_loop(0, EARLY, early_tile, 0)
    gather_q.third()

    def arrive(i):
        even = lax.rem(i, 2) == 0

        @pl.when(i == 2)
        def _():
            gather_q.wait(gather_q.side_own())

        @pl.when((i >= 4) & (i < 12) & even)
        def _():
            gather_q.pass_near(lax.div(i, 2) - 2)

        @pl.when((i >= 4) & (i < 12) & jnp.logical_not(even))
        def _():
            gather_q.wait(gather_q.side_near(lax.div(i, 2) - 2))

        @pl.when((i >= 12) & even)
        def _():
            gather_q.pass_far(lax.div(i, 2) - 6)
            gather_q.pass_far(lax.div(i, 2) - 4)

        @pl.when((i >= 12) & jnp.logical_not(even))
        def _():
            gather_q.wait(gather_q.side_far(lax.div(i, 2) - 6))
            gather_q.wait(gather_q.side_far(lax.div(i, 2) - 4))

    def early_step(i, total):
        arrive(i)
        return total + dot(chunk_vectors(i), pre_ref[i], ((1,), (0,)))

    total = lax.fori_loop(0, EARLY, early_step, jnp.zeros((RANK, OWN), f32))

    def sketch_step(i, total):
        arrive(i)
        tile = chunk_tile(i)
        return total + dot(chunk_vectors(i), tile, ((1,), (0,)))

    narrow = lax.fori_loop(EARLY, 16, sketch_step, total)

    stacked = jnp.concatenate([narrow[:, :LEAF], narrow[:, LEAF:]], axis=0)
    left = lax.broadcasted_iota(jnp.int32, (1, 2 * RANK), 1) < RANK
    root, scale = inverse_root(stacked, left)
    scale = jnp.sqrt(scale)
    rounded = (dot(stacked, root, ((0,), (0,)), HIGHEST) / scale).astype(bf16)
    for unit, row in enumerate(gather_b.own_rows()):
        for n in range(2):
            at = unit * RANK + LINES * n
            b_ref[row + n] = rounded[at : at + LINES, :]
    gather_b.start(gather_b.first(0))

    packed = rounded.astype(f32)
    sc_ref[...] = packed
    flipped = packed.T
    for side in range(2):
        sct_ref[128 * side : 128 * (side + 1), :] = flipped[:, 128 * side : 128 * (side + 1)]
    even, odd = sc_ref[pl.ds(0, 128, stride=2), :], sc_ref[pl.ds(1, 128, stride=2), :]
    sc_ref[:128, :] = jnp.where(left, even, pltpu.roll(odd, RANK, 1))
    sc_ref[128:, :] = jnp.where(left, pltpu.roll(even, RANK, 1), odd)
    for i in range(128):
        bases_out[:, 128 * i : 128 * (i + 1)] = sc_ref[pl.ds(i, 2, stride=128), :].astype(bf16)
    half = RANK // 2
    for leaf in range(2):
        for odd_one in range(2):
            at = odd_one * half
            for side in range(2):
                first = 128 * side + leaf * RANK + odd_one
                bs_ref[leaf, at : at + half, 128 * side : 128 * (side + 1)] = sct_ref[
                    pl.ds(first, half, stride=2), :
                ].astype(bf16)

    def near_step(g, carry):
        @pl.when(g == 5)
        def _():
            gather_b.second()

        far = []
        for n in range(GROUP):
            entry = (owners[0, g * GROUP + n] * 2 + picks[1, g * GROUP + n]) * 2
            far += [x_ref[entry], x_ref[entry + 1]]
        far = features(jnp.concatenate(far, axis=1), True)
        tiles = []
        for n in range(GROUP):
            near_rows = gt_ref[picks[0, g * GROUP + n]]
            exponent = dot(near_rows, far[:, n * LEAF : (n + 1) * LEAF], ((1,), (0,)))
            tiles.append(jnp.exp2(exponent).astype(bf16))
        for n, tile in enumerate(tiles):
            k = g * GROUP + n
            rows = pl.ds(pl.multiple_of(k * RANK, RANK), RANK)
            pre_ref[0, rows, :LEAF] = dot(bs_ref[picks[0, k]], tile, ((1,), (0,))).astype(bf16)
        return carry

    lax.fori_loop(0, PAIRS // GROUP, near_step, 0)

    gather_b.third()

    def near_planes(r, carry):
        gather_b.pass_near(r)
        return carry

    def far_planes(r, carry):
        gather_b.pass_far(r)
        return carry

    def siblings(r, carry):
        gather_b.wait(gather_b.side_near(r))
        gather_b.wait(gather_b.side_far(r))
        return carry

    lax.fori_loop(0, 4, near_planes, 0)
    lax.fori_loop(0, 4, far_planes, 0)
    gather_b.wait(gather_b.side_own())
    lax.fori_loop(0, 4, siblings, 0)

    def far_step(g, carry):
        products = []
        for pair in range(GROUP):
            k = g * GROUP + pair
            line, col = lax.div(owners[0, k], 16), lax.rem(owners[0, k], 16)
            core, z = lax.rem(line, 2), lax.div(line, 2)
            x, y = lax.div(col, SIDE), lax.rem(col, SIDE)
            slots = [z * 16 + y * 4 + x, x * 16 + z * 4 + y, y * 16 + x * 4 + z]
            blocks = []
            for part in range(3):
                slot = slots[part] + core * (slots[(part + 1) % 3] - slots[part])
                row = core * (CORE_ROWS // LINES) + PART_BASE[part] // LINES + slot * (PART_ROWS[part] // LINES)
                for n in range(PART_ROWS[part] // LINES):
                    blocks.append(b_ref[row + n])
            rows = pl.ds(pl.multiple_of(k * RANK, RANK), RANK)
            near = pre_ref[0, rows, :LEAF]
            products.append(dot(near, jnp.concatenate(blocks, axis=0), ((1,), (0,))))
        for pair, both in enumerate(products):
            k = g * GROUP + pair
            even, odd = both[:half, :], both[half:, :]
            first = jnp.where(left, even, pltpu.roll(odd, RANK, 1))
            second = jnp.where(left, pltpu.roll(even, RANK, 1), odd)
            pick = picks[1, k].astype(f32)
            st_ref[pair * half : (pair + 1) * half, :] = first * (1.0 - pick) + second * pick
        rows = pl.ds(pl.multiple_of(g * GROUP, GROUP), GROUP)
        for i in range(half):
            coup_out[rows, 128 * i : 128 * (i + 1)] = st_ref[pl.ds(i, GROUP, stride=half), :]
        return carry

    lax.fori_loop(0, PAIRS // GROUP, far_step, 0)
    gather_q.finish_sends()
    gather_b.finish_sends()


def per_device(coords, panel, mixing, owners, leaf_picks):
    vmem = pl.BlockSpec(memory_space=pltpu.VMEM)
    smem = pl.BlockSpec(memory_space=pltpu.SMEM)
    sems = pltpu.SemaphoreType.DMA
    points = coords.shape[1]
    bases, couplings = pl.pallas_call(
        kernel,
        out_shape=(
            pltpu.VMEM((2, LEAF * RANK), bf16),
            pltpu.VMEM((PAIRS, RANK * RANK), f32),
        ),
        in_specs=[pl.BlockSpec(memory_space=pl.ANY), vmem, vmem, smem, smem],
        out_specs=(vmem, vmem),
        scratch_shapes=[
            pltpu.VMEM((4, coords.shape[0], points // INPUTS), f32),
            pltpu.VMEM((points // UNIT, coords.shape[0], UNIT), f32),
            pltpu.VMEM((EARLY, CHUNK, OWN), bf16),
            pltpu.VMEM((2 * CORE_ROWS // LINES, LINES, 128), bf16),
            pltpu.VMEM((2 * CORE_ROWS // LINES, LINES, 128), bf16),
            pltpu.VMEM((128, OWN), bf16),
            pltpu.VMEM((2, LEAF, 128), bf16),
            pltpu.VMEM((2, RANK, LEAF), bf16),
            pltpu.VMEM((LEAF, 128), f32),
            pltpu.VMEM((2 * 128, 128), f32),
            pltpu.VMEM((GROUP * RANK // 2, 128), f32),
            sems((4,)),
            sems((3, 18)),
            sems((3, 18)),
            sems((3, 13)),
            sems((3, 13)),
            sems((3, 18)),
            sems((3, 18)),
            sems((3, 13)),
            sems((3, 13)),
        ],
        compiler_params=pltpu.CompilerParams(
            collective_id=0, has_side_effects=True, vmem_limit_bytes=60 * 2**20
        ),
    )(coords, panel, mixing.T, owners.T, leaf_picks.T)
    return bases, couplings


def solution(mesh):
    return jax.shard_map(
        per_device,
        mesh=mesh,
        in_specs=(
            P(),
            P(("row", "col"), None),
            P(),
            P(("row", "col"), None),
            P(("row", "col"), None),
        ),
        out_specs=(P(("row", "col"), None), P(("row", "col"), None)),
        check_vma=False,
    )
```

```python
import functools
import math

import jax
import jax.numpy as jnp
from jax import lax
from jax.experimental import pallas as pl
from jax.experimental.pallas import tpu as pltpu
from jax.sharding import PartitionSpec as P

MESH = pl.DeviceIdType.MESH
HIGHEST = lax.Precision.HIGHEST
f32, bf16 = jnp.float32, jnp.bfloat16

LEAF = 256
RANK = 64
NSWEEPS = 6
EPSILON = 1e-06
OWN = 512
UNIT = 128
UNITS = 4
PAIRS = 64
GROUP = 8
LINES = 32
SIDE = 4
CHUNK = 4096
EARLY = 6
INPUTS = 16
PART_UNITS = (2, 1, 1)
PART_ROWS = tuple(RANK * u for u in PART_UNITS)
PART_BASE = (0, 128 * SIDE**3, 192 * SIDE**3)
CORE_ROWS = 256 * SIDE**3


def dot(a, b, dims, precision=None):
    return lax.dot_general(
        a, b, (dims, ((), ())), precision=precision, preferred_element_type=f32
    )


def pick3(k, a, b, c):
    return jnp.where(k == 0, a, jnp.where(k == 1, b, c))


def back(j):
    return jnp.where(j == 0, 0, lax.rem(j, 3) + 1)


def split3(v):
    hi = v.astype(bf16)
    rest = v - hi.astype(f32)
    mid = rest.astype(bf16)
    lo = (rest - mid.astype(f32)).astype(bf16)
    return hi, mid, lo


def features(x, column):
    n = x.shape[1]
    a = x * math.sqrt(4.0 * math.log2(math.e) / x.shape[0])
    h = -0.5 * jnp.sum(a * a, axis=0, keepdims=True)
    hi, mid, lo = split3(a)
    parts = [jnp.broadcast_to(v.astype(f32), (16, n)) for v in split3(h)]
    line = lax.broadcasted_iota(jnp.int32, (16, n), 0)
    at = 0 if column else 3
    extra = jnp.where(line < 6, 1.0, 0.0)
    for k in range(3):
        extra = jnp.where(line == at + k, parts[k], extra)
    extra = extra.astype(bf16)
    zero = jnp.zeros((16, n), bf16)
    if column:
        stack = [hi, hi, mid, mid, hi, lo, extra, zero]
    else:
        stack = [hi, mid, hi, mid, lo, hi, extra, zero]
    return jnp.concatenate(stack, axis=0)


class Place:
    def __init__(self):
        row, col = lax.axis_index("row"), lax.axis_index("col")
        self.core = lax.rem(row, 2)
        self.z = lax.div(row, 2)
        self.x = lax.div(col, SIDE)
        self.y = lax.rem(col, SIDE)
        self.index = row * SIDE * SIDE + col

    def sibling(self):
        return (self.z * 2 + 1 - self.core, self.x * SIDE + self.y)

    def neighbour(self, axis, step):
        x = lax.rem(self.x + jnp.where(axis == 0, step, 0), SIDE)
        y = lax.rem(self.y + jnp.where(axis == 1, step, 0), SIDE)
        z = lax.rem(self.z + jnp.where(axis == 2, step, 0), SIDE)
        return (z * 2 + self.core, x * SIDE + y)

    def along(self, turn):
        c = (self.x, self.y, self.z)
        return [pick3(turn, c[s], c[(s + 1) % 3], c[(s + 2) % 3]) for s in range(3)]


class Gather:
    def __init__(self, place, buf, send, recv, sib_send, sib_recv):
        self.place, self.buf = place, buf
        self.send, self.recv = send, recv
        self.sib_send, self.sib_recv = sib_send, sib_recv

    def turn(self, part):
        return lax.rem(part + self.place.core, 3)

    def start_row(self, part, slot):
        return self.place.core * CORE_ROWS + PART_BASE[part] + slot * PART_ROWS[part]

    def ref(self, part, plane, group, slot, slots):
        first = lax.rem(plane, SIDE) * 16 + lax.rem(group, SIDE) * 4 + slot
        start = lax.div(self.start_row(part, first), LINES)
        return self.buf.at[pl.ds(start, slots * PART_ROWS[part] // LINES)]

    def copy(self, part, stage, ref, step, sem):
        return pltpu.make_async_remote_copy(
            src_ref=ref,
            dst_ref=ref,
            send_sem=self.send.at[part, sem],
            recv_sem=self.recv.at[part, sem],
            device_id=self.place.neighbour(lax.rem(self.turn(part) + stage, 3), step),
            device_id_type=MESH,
        )

    def first(self, stage):
        result = []
        for part in range(3):
            u = self.place.along(self.turn(part))
            ref = self.ref(part, u[2], u[1], u[0] if stage == 0 else 0, 1 if stage == 0 else 4)
            result += [self.copy(part, stage, ref, s, 3 * stage + s - 1) for s in (1, 2, 3)]
        return result

    def near_plane(self, j):
        result = []
        for part in range(3):
            u = self.place.along(self.turn(part))
            for way, (r, s) in enumerate(((j, 1), (back(j), SIDE - 1))):
                ref = self.ref(part, u[2], u[1] + r, 0, 4)
                result.append(self.copy(part, 2, ref, s, 6 + 2 * j + way))
        return result

    def far_plane(self, r):
        step = 1 + 2 * lax.div(r, 2)
        result = []
        for part in range(3):
            u = self.place.along(self.turn(part))
            ref = self.ref(part, u[2] + SIDE - step, u[1] + r, 0, 4)
            result.append(self.copy(part, 2, ref, step, 14 + r))
        return result

    def side(self, ref, part, sem):
        return pltpu.make_async_remote_copy(
            src_ref=ref,
            dst_ref=ref,
            send_sem=self.sib_send.at[part, sem],
            recv_sem=self.sib_recv.at[part, sem],
            device_id=self.place.sibling(),
            device_id_type=MESH,
        )

    def side_own(self):
        result = []
        for part in range(3):
            u = self.place.along(self.turn(part))
            result.append(self.side(self.ref(part, u[2], 0, 0, 16), part, 0))
        return result

    def side_near(self, j):
        result = []
        for part in range(3):
            u = self.place.along(self.turn(part))
            for way, (r, plane) in enumerate(((j, 3), (back(j), 1))):
                ref = self.ref(part, u[2] + plane, u[1] + r, 0, 4)
                result.append(self.side(ref, part, 1 + 2 * j + way))
        return result

    def side_far(self, r):
        result = []
        for part in range(3):
            u = self.place.along(self.turn(part))
            result.append(self.side(self.ref(part, u[2] + 2, u[1] + r, 0, 4), part, 9 + r))
        return result

    def start(self, copies):
        for copy in copies:
            copy.start()

    def wait(self, copies):
        for copy in copies:
            copy.wait_recv()

    def second(self):
        self.wait(self.first(0))
        self.start(self.first(1))
        self.start(self.near_plane(0))

    def third(self):
        self.wait(self.first(1))
        for r in range(1, 4):
            self.start(self.near_plane(r))
        self.start(self.side_own())

    def pass_near(self, j):
        self.wait(self.near_plane(j))
        for r, when in enumerate((0, 1, 1, 2)):

            @pl.when(j == when)
            def _(r=r):
                self.start(self.far_plane(r))

        self.start(self.side_near(j))

    def pass_far(self, r):
        self.wait(self.far_plane(r))
        self.start(self.side_far(r))

    def own_rows(self):
        rows = []
        for part in range(3):
            u = self.place.along(self.turn(part))
            start = self.start_row(part, u[2] * 16 + u[1] * 4 + u[0])
            for unit in range(PART_UNITS[part]):
                rows.append(lax.div(start + unit * RANK, LINES))
        return rows

    def finish_sends(self):
        for copy in self.first(0) + self.first(1) + self.side_own():
            copy.wait_send()

        def step(r, carry):
            copies = self.near_plane(r) + self.far_plane(r) + self.side_near(r) + self.side_far(r)
            for copy in copies:
                copy.wait_send()
            return carry

        lax.fori_loop(0, 4, step, 0)


def dot3(a, b):
    ah, bh = a.astype(bf16), b.astype(bf16)
    al, bl = (a - ah.astype(f32)).astype(bf16), (b - bh.astype(f32)).astype(bf16)
    by = ((1,), (0,))
    return dot(ah, bh, by) + (dot(ah, bl, by) + dot(al, bh, by))


def inverse_root(stacked, left):
    shape = (2 * RANK, 2 * RANK)
    row = lax.broadcasted_iota(jnp.int32, shape, 0)
    col = lax.broadcasted_iota(jnp.int32, shape, 1)
    gram = jnp.where((row < RANK) == (col < RANK), dot(stacked, stacked, ((1,), (1,)), HIGHEST), 0.0)
    sums = jnp.sum(gram * gram, axis=0, keepdims=True)
    zero = jnp.zeros_like(sums)
    sums = [jnp.sum(v, axis=1, keepdims=True) for v in (jnp.where(left, sums, zero), jnp.where(left, zero, sums))]
    scale = jnp.sqrt(jnp.where(left, sums[0], sums[1]) + EPSILON)
    iterate = gram / scale
    ident = jnp.where(row == col, 1.0, 0.0)
    root = ident
    for sweep in range(NSWEEPS):
        product = iterate if sweep == 0 else dot3(root, iterate)
        factor = 1.5 * ident - 0.5 * product
        if sweep < NSWEEPS - 1:
            iterate = dot3(iterate, factor)
        root = factor if sweep == 0 else dot3(factor, root)
    return root, scale


def kernel(
    coords, panel, mixing, owners, picks, bases_out, coup_out,
    in_ref, x_ref, pre_ref, q_ref, b_ref, g_ref, gt_ref, l_ref, bs_ref, sc_ref, sct_ref, st_ref,
    in_sem, q_send, q_recv, q_sib_send, q_sib_recv, b_send, b_recv, b_sib_send, b_sib_recv,
):
    place = Place()
    gather_q = Gather(place, q_ref, q_send, q_recv, q_sib_send, q_sib_recv)
    gather_b = Gather(place, b_ref, b_send, b_recv, b_sib_send, b_sib_recv)

    width = coords.shape[1] // INPUTS

    def load(j):
        return pltpu.make_async_copy(
            coords.at[:, j * width : (j + 1) * width], in_ref.at[j % 4], in_sem.at[j % 4]
        )

    for j in range(4):
        load(j).start()
    barrier = pltpu.get_barrier_semaphore()
    peers = [place.neighbour(axis, step) for axis in range(3) for step in (1, 2, 3)]
    peers.append(place.sibling())
    for peer in peers:
        pl.semaphore_signal(barrier, inc=1, device_id=peer, device_id_type=MESH)

    vectors = dot(mixing[...], panel[...].astype(f32), ((1,), (1,)), HIGHEST).astype(bf16)
    for unit, row in enumerate(gather_q.own_rows()):
        for n in range(2):
            q_ref[row + n] = vectors[LINES * n : LINES * (n + 1), unit * UNIT : (unit + 1) * UNIT]
    for j in range(INPUTS):
        load(j).wait()
        for unit in range(width // UNIT):
            x_ref[j * width // UNIT + unit] = in_ref[j % 4, :, unit * UNIT : (unit + 1) * UNIT]
        if j + 4 < INPUTS:
            load(j + 4).start()
    own = [x_ref[place.index * UNITS + unit] for unit in range(UNITS)]
    own_features = features(jnp.concatenate(own, axis=1), False)
    g_ref[...] = own_features
    for leaf in range(2):
        gt_ref[leaf] = own_features[:, leaf * LEAF : (leaf + 1) * LEAF].T

    pl.semaphore_wait(barrier, len(peers))

    gather_q.start(gather_q.first(0))
    def chunk(i):
        in_own, in_far = i < 4, i >= 12
        other = jnp.where(in_own, lax.div(i, 2), lax.rem(i, 2))
        core = lax.rem(place.core + other, 2)
        r = jnp.where(in_far, lax.div(i + 4, 2) - 8, jnp.where(in_own, 2 * lax.rem(i, 2), lax.div(i, 2) - 2))
        groups = (r, jnp.where(in_far, r + 2, jnp.where(in_own, r + 1, back(r))))
        planes = [jnp.where(in_far, 2, jnp.where(in_own, 0, p)) for p in (3, 1)]
        units = []
        for half in range(2):
            for unit in range(UNITS):
                part = max(unit - 1, 0)
                turn = lax.rem(part + core, 3)
                w = [pick3(turn, *((4, 1, 32) * 2)[s : s + 3]) for s in range(3)]
                u = place.along(turn)
                u2, u1 = lax.rem(u[2] + planes[half], SIDE), lax.rem(u[1] + groups[half], SIDE)
                device = core * 16 + u2 * w[2] + u1 * w[1]
                entry = core * (CORE_ROWS // LINES) + PART_BASE[part] // LINES
                size = PART_ROWS[part] // LINES
                entry = entry + (u2 * 16 + u1 * 4) * size + (unit % 2 if part == 0 else 0) * 2
                for u0 in range(SIDE):
                    units.append(((device + u0 * w[0]) * UNITS + unit, entry + u0 * size))
        return units

    def chunk_tile(i):
        columns = features(jnp.concatenate([x_ref[p] for p, _ in chunk(i)], axis=1), True).T
        return jnp.exp2(dot(columns, g_ref[...], ((1,), (0,)))).astype(bf16)

    def chunk_vectors(i):
        vectors = [jnp.concatenate([q_ref[v], q_ref[v + 1]], axis=0) for _, v in chunk(i)]
        return jnp.concatenate(vectors, axis=1)

    def early_tile(i, carry):
        @pl.when(i == 3)
        def _():
            gather_q.second()

        pre_ref[i] = chunk_tile(i)
        return carry

    lax.fori_loop(0, EARLY, early_tile, 0)
    gather_q.third()

    def arrive(i):
        even = lax.rem(i, 2) == 0

        @pl.when(i == 2)
        def _():
            gather_q.wait(gather_q.side_own())

        @pl.when((i >= 4) & (i < 12) & even)
        def _():
            gather_q.pass_near(lax.div(i, 2) - 2)

        @pl.when((i >= 4) & (i < 12) & jnp.logical_not(even))
        def _():
            gather_q.wait(gather_q.side_near(lax.div(i, 2) - 2))

        @pl.when((i >= 12) & even)
        def _():
            gather_q.pass_far(lax.div(i, 2) - 6)
            gather_q.pass_far(lax.div(i, 2) - 4)

        @pl.when((i >= 12) & jnp.logical_not(even))
        def _():
            gather_q.wait(gather_q.side_far(lax.div(i, 2) - 6))
            gather_q.wait(gather_q.side_far(lax.div(i, 2) - 4))

    def early_step(i, total):
        arrive(i)
        return total + dot(chunk_vectors(i), pre_ref[i], ((1,), (0,)))

    total = lax.fori_loop(0, EARLY, early_step, jnp.zeros((RANK, OWN), f32))

    def sketch_step(i, total):
        arrive(i)
        tile = chunk_tile(i)
        return total + dot(chunk_vectors(i), tile, ((1,), (0,)))

    narrow = lax.fori_loop(EARLY, 16, sketch_step, total)

    stacked = jnp.concatenate([narrow[:, :LEAF], narrow[:, LEAF:]], axis=0)
    left = lax.broadcasted_iota(jnp.int32, (1, 2 * RANK), 1) < RANK
    root, scale = inverse_root(stacked, left)
    scale = jnp.sqrt(scale)
    rounded = (dot(stacked, root, ((0,), (0,)), HIGHEST) / scale).astype(bf16)
    for unit, row in enumerate(gather_b.own_rows()):
        for n in range(2):
            at = unit * RANK + LINES * n
            b_ref[row + n] = rounded[at : at + LINES, :]
    gather_b.start(gather_b.first(0))

    packed = rounded.astype(f32)
    sc_ref[...] = packed
    flipped = packed.T
    for side in range(2):
        sct_ref[128 * side : 128 * (side + 1), :] = flipped[:, 128 * side : 128 * (side + 1)]
    even, odd = sc_ref[pl.ds(0, 128, stride=2), :], sc_ref[pl.ds(1, 128, stride=2), :]
    sc_ref[:128, :] = jnp.where(left, even, pltpu.roll(odd, RANK, 1))
    sc_ref[128:, :] = jnp.where(left, pltpu.roll(even, RANK, 1), odd)
    for i in range(128):
        bases_out[:, 128 * i : 128 * (i + 1)] = sc_ref[pl.ds(i, 2, stride=128), :].astype(bf16)
    half = RANK // 2
    for leaf in range(2):
        for odd_one in range(2):
            at = odd_one * half
            for side in range(2):
                first = 128 * side + leaf * RANK + odd_one
                bs_ref[leaf, at : at + half, 128 * side : 128 * (side + 1)] = sct_ref[
                    pl.ds(first, half, stride=2), :
                ].astype(bf16)

    def near_step(g, carry):
        @pl.when(g == 5)
        def _():
            gather_b.second()

        far = []
        for n in range(GROUP):
            entry = (owners[0, g * GROUP + n] * 2 + picks[1, g * GROUP + n]) * 2
            far += [x_ref[entry], x_ref[entry + 1]]
        far = features(jnp.concatenate(far, axis=1), True)
        tiles = []
        for n in range(GROUP):
            near_rows = gt_ref[picks[0, g * GROUP + n]]
            exponent = dot(near_rows, far[:, n * LEAF : (n + 1) * LEAF], ((1,), (0,)))
            tiles.append(jnp.exp2(exponent).astype(bf16))
        for n, tile in enumerate(tiles):
            k = g * GROUP + n
            l_ref[k] = dot(bs_ref[picks[0, k]], tile, ((1,), (0,))).astype(bf16)
        return carry

    lax.fori_loop(0, PAIRS // GROUP, near_step, 0)

    gather_b.third()

    def near_planes(r, carry):
        gather_b.pass_near(r)
        return carry

    def far_planes(r, carry):
        gather_b.pass_far(r)
        return carry

    def siblings(r, carry):
        gather_b.wait(gather_b.side_near(r))
        gather_b.wait(gather_b.side_far(r))
        return carry

    lax.fori_loop(0, 4, near_planes, 0)
    lax.fori_loop(0, 4, far_planes, 0)
    gather_b.wait(gather_b.side_own())
    lax.fori_loop(0, 4, siblings, 0)

    def far_step(g, carry):
        for pair in range(GROUP):
            k = g * GROUP + pair
            line, col = lax.div(owners[0, k], 16), lax.rem(owners[0, k], 16)
            core, z = lax.rem(line, 2), lax.div(line, 2)
            x, y = lax.div(col, SIDE), lax.rem(col, SIDE)
            slots = [z * 16 + y * 4 + x, x * 16 + z * 4 + y, y * 16 + x * 4 + z]
            blocks = []
            for part in range(3):
                slot = slots[part] + core * (slots[(part + 1) % 3] - slots[part])
                row = core * (CORE_ROWS // LINES) + PART_BASE[part] // LINES + slot * (PART_ROWS[part] // LINES)
                for n in range(PART_ROWS[part] // LINES):
                    blocks.append(b_ref[row + n])
            both = dot(
                l_ref[k],
                jnp.concatenate(blocks, axis=0),
                ((1,), (0,)),
            )
            even, odd = both[:half, :], both[half:, :]
            first = jnp.where(left, even, pltpu.roll(odd, RANK, 1))
            second = jnp.where(left, pltpu.roll(even, RANK, 1), odd)
            pick = picks[1, k].astype(f32)
            st_ref[pair * half : (pair + 1) * half, :] = first * (1.0 - pick) + second * pick
        rows = pl.ds(pl.multiple_of(g * GROUP, GROUP), GROUP)
        for i in range(half):
            coup_out[rows, 128 * i : 128 * (i + 1)] = st_ref[pl.ds(i, GROUP, stride=half), :]
        return carry

    lax.fori_loop(0, PAIRS // GROUP, far_step, 0)
    gather_q.finish_sends()
    gather_b.finish_sends()


def per_device(coords, panel, mixing, owners, leaf_picks):
    vmem = pl.BlockSpec(memory_space=pltpu.VMEM)
    smem = pl.BlockSpec(memory_space=pltpu.SMEM)
    sems = pltpu.SemaphoreType.DMA
    points = coords.shape[1]
    bases, couplings = pl.pallas_call(
        kernel,
        out_shape=(
            pltpu.VMEM((2, LEAF * RANK), bf16),
            pltpu.VMEM((PAIRS, RANK * RANK), f32),
        ),
        in_specs=[pl.BlockSpec(memory_space=pl.ANY), vmem, vmem, smem, smem],
        out_specs=(vmem, vmem),
        scratch_shapes=[
            pltpu.VMEM((4, coords.shape[0], points // INPUTS), f32),
            pltpu.VMEM((points // UNIT, coords.shape[0], UNIT), f32),
            pltpu.VMEM((EARLY, CHUNK, OWN), bf16),
            pltpu.VMEM((2 * CORE_ROWS // LINES, LINES, 128), bf16),
            pltpu.VMEM((2 * CORE_ROWS // LINES, LINES, 128), bf16),
            pltpu.VMEM((128, OWN), bf16),
            pltpu.VMEM((2, LEAF, 128), bf16),
            pltpu.VMEM((PAIRS, RANK, LEAF), bf16),
            pltpu.VMEM((2, RANK, LEAF), bf16),
            pltpu.VMEM((LEAF, 128), f32),
            pltpu.VMEM((2 * 128, 128), f32),
            pltpu.VMEM((GROUP * RANK // 2, 128), f32),
            sems((4,)),
            sems((3, 18)),
            sems((3, 18)),
            sems((3, 13)),
            sems((3, 13)),
            sems((3, 18)),
            sems((3, 18)),
            sems((3, 13)),
            sems((3, 13)),
        ],
        compiler_params=pltpu.CompilerParams(
            collective_id=0, has_side_effects=True, vmem_limit_bytes=60 * 2**20
        ),
    )(coords, panel, mixing.T, owners.T, leaf_picks.T)
    return bases, couplings


def solution(mesh):
    return jax.shard_map(
        per_device,
        mesh=mesh,
        in_specs=(
            P(),
            P(("row", "col"), None),
            P(),
            P(("row", "col"), None),
            P(("row", "col"), None),
        ),
        out_specs=(P(("row", "col"), None), P(("row", "col"), None)),
        check_vma=False,
    )
```
